256 devices in a mesh: dp: 32 (over z, y), ctx: 4 (over x), side: 2 (over core).
Axes of the slice: x: 4, y: 4, z: 8, core: 2. Of those that a mesh axis runs over, the one named last changes fastest.
Arguments:
- queries: bfloat16 [64, 8192], P('dp'), may hold values from -70 to 70
- new_key: bfloat16 [64, 1024], P('dp'), may hold values from -40 to 40
- new_value: bfloat16 [64, 1024], P('dp'), may hold values from -6 to 6
- key_pool: bfloat16 [6144, 64, 1024], P(('dp', 'ctx', 'side')), may hold values from -40 to 40
- value_pool: bfloat16 [6144, 64, 1024], P(('dp', 'ctx', 'side')), may hold values from -6 to 6
- page_table: int32 [32, 8, 24], P('dp', ('ctx', 'side')), may hold values from 0 to 23, each once within a row
- lengths: int32 [64], P('dp'), may hold values from 1 to 6144, as said below
- residual: bfloat16 [64, 8192], P(None, 'dp'), may hold values from -40 to 40
- out_weight: bfloat16 [8192, 8192], P(('ctx', 'side'), 'dp'), may hold values from -0.5 to 0.5
- norm_gain: float32 [8192], P('dp'), may hold values from 0.1 to 1.9
- gate_weight: bfloat16 [8192, 28672], P('dp', ('ctx', 'side')), may hold values from -0.0625 to 0.0625
- up_weight: bfloat16 [8192, 28672], P('dp', ('ctx', 'side')), may hold values from -0.0625 to 0.0625
- down_weight: bfloat16 [28672, 8192], P(('ctx', 'side'), 'dp'), may hold values from -0.03125 to 0.03125
Outputs:
- layer_out: bfloat16 [64, 8192], P(('ctx', 'side'), 'dp')
The draws below stay inside these ranges and needn't reach their ends.
Inputs may be any that keep to these rules, and one draw needn't show every extreme that they name: `lengths`: cached tokens of each row; the new token comes after them.
All inputs are finite; a program needn't handle non-finite values.
Results may differ from the reference program's by a relative error of at most 0.018.
Values may be sent and summed in bfloat16 or wider, within the bound.
No kernel may reach another device: no remote copies, remote signals or barrier semaphores. Data moves between devices by JAX's collectives and lax.ppermute only.
A program may use at most 64 MiB of HBM per device.

```python
import math
import jax
import jax.numpy as jnp
from jax import lax

D = 8192
H = 64
KVH = 8
HD = 128
FF = 28672
ROWS_DEV = 2
PAGE = 64
PMAX = 12
NSH = 8
G = 8
ROWS = 64
PAGES_DEV = 24
POOL = 6144
MAXLEN = 6144
N_DP = 32


def draw_queries(key, part):
    key = jax.random.fold_in(key, 3)
    drawn = 1.5 * jnp.clip(jax.random.normal(key, (ROWS, KVH, G, HD), jnp.float32), -6.0, 6.0)
    return drawn.reshape(ROWS, H * HD).astype(jnp.bfloat16)


def draw_new_key(key, part):
    key = jax.random.fold_in(key, 5)
    drawn = jnp.clip(jax.random.normal(key, (ROWS, KVH, HD), jnp.float32), -6.0, 6.0)
    return drawn.reshape(ROWS, KVH * HD).astype(jnp.bfloat16)


def draw_key_pool(key, part):
    key = jax.random.fold_in(key, 7)
    drawn = jnp.clip(jax.random.normal(key, (POOL, PAGE, KVH, HD), jnp.float32), -6.0, 6.0)
    return drawn.reshape(POOL, PAGE, KVH * HD).astype(jnp.bfloat16)


def draw_lengths(key, part):
    key = jax.random.fold_in(key, 9)
    groups = ROWS // ROWS_DEV
    factor = jax.random.randint(jax.random.fold_in(key, 1), (groups, 1), 1, 4)
    ceiling = MAXLEN * factor // 3
    drawn = 1 + jax.random.randint(jax.random.fold_in(key, 2), (groups, ROWS_DEV), 0, ceiling)
    flat_rows = drawn.reshape(ROWS)
    chosen = jax.random.randint(jax.random.fold_in(key, 3), (), 0, ROWS)
    return jnp.where(jnp.arange(ROWS) == chosen, MAXLEN, flat_rows).astype(jnp.int32)


def draw_residual(key, part):
    key = jax.random.fold_in(key, 11)
    row_scale = jnp.exp(jax.random.uniform(jax.random.fold_in(key, 1), (ROWS, 1), jnp.float32, math.log(0.3), math.log(3.0)))
    ramp = 1.0 + 2.0 * jnp.arange(D, dtype=jnp.float32)[None, :] / D
    col_scale = jnp.exp(jax.random.uniform(jax.random.fold_in(key, 2), (1, D), jnp.float32, math.log(0.5), math.log(2.0))) * ramp
    noise = jnp.clip(jax.random.normal(jax.random.fold_in(key, 3), (ROWS, D), jnp.float32), -6.0, 6.0)
    return (0.1 * noise * row_scale * col_scale).astype(jnp.bfloat16)


def levels(own_key, shape, pieces, low, top_value):
    factor_of = 1.0
    for axis_at, blocks in pieces:
        heights = jax.random.uniform(jax.random.fold_in(jax.random.fold_in(own_key, 6), axis_at), (blocks,), jnp.float32, low / len(pieces), top_value / len(pieces))
        factor_of = factor_of * jnp.repeat(jnp.exp(heights), shape[axis_at] // blocks).reshape((-1,) + (1,) * (len(shape) - 1 - axis_at))
    return factor_of


def bell_draw(own_key, shape, width, limit, shards=(), held_as=jnp.bfloat16):
    result = jax.random.normal(own_key, shape, jnp.float32) * width
    if len(shards) > 0:
        result = levels(own_key, shape, shards, -0.22, 0.18) * result
    return jnp.clip(result, min=-limit, max=limit).astype(held_as)


def setup_inputs(seed: int = 0) -> dict:
    key_of = jax.random.split(jax.random.key(seed), 14)
    return {
        "queries": draw_queries(jax.random.fold_in(key_of[13], 71), 0),
        "new_key": draw_new_key(jax.random.fold_in(key_of[13], 71), 0),
        "new_value": bell_draw(key_of[2], (ROWS, KVH * HD), 1.0, 6.0, ((0, 32),)),
        "key_pool": draw_key_pool(jax.random.fold_in(key_of[13], 71), 0),
        "value_pool": bell_draw(key_of[4], (POOL, PAGE, KVH * HD), 1.0, 6.0, ((0, 256),)),
        "page_table": jax.vmap(lambda own: jax.random.permutation(own, PAGES_DEV))(jax.random.split(key_of[5], N_DP * NSH)).reshape((N_DP, NSH, PAGES_DEV)).astype(jnp.int32),
        "lengths": draw_lengths(jax.random.fold_in(key_of[13], 71), 0),
        "residual": draw_residual(jax.random.fold_in(key_of[13], 71), 0),
        "out_weight": bell_draw(key_of[8], (H * HD, D), (H * HD // 64) ** -0.5, 0.5, ((0, 8), (1, 32))),
        "norm_gain": jnp.clip(1.0 + 0.18 * jax.random.normal(key_of[9], (D,), jnp.float32), 0.1, 1.9),
        "gate_weight": bell_draw(key_of[10], (D, FF), D ** -0.5, 0.0625, ((0, 32), (1, 8))),
        "up_weight": bell_draw(key_of[11], (D, FF), D ** -0.5, 0.0625, ((0, 32), (1, 8))),
        "down_weight": bell_draw(key_of[12], (FF, D), FF ** -0.5, 0.03125, ((0, 8), (1, 32))),
    }


def gather_row(pool, page_table, row_index):
    block_index = row_index // ROWS_DEV
    local_index = row_index % ROWS_DEV
    logical = jnp.arange(NSH * PMAX, dtype=jnp.int32)
    shard_ids = logical % NSH
    within = logical // NSH
    slot_ids = page_table[block_index, shard_ids, local_index * PMAX + within].astype(jnp.int32)
    pool_index = (block_index * NSH + shard_ids) * PAGES_DEV + slot_ids
    return pool[pool_index].reshape(MAXLEN, KVH, HD)

def reference(queries, new_key, new_value, key_pool, value_pool, page_table, lengths, residual, out_weight, norm_gain, gate_weight, up_weight, down_weight):
    score_scale = 1.0 / math.sqrt(HD)

    def attend(row_index):
        query_row = queries[row_index].astype(jnp.float32).reshape(KVH, G, HD)
        fresh_key = new_key[row_index].astype(jnp.float32).reshape(KVH, HD)
        fresh_value = new_value[row_index].astype(jnp.float32).reshape(KVH, HD)
        cached_keys = gather_row(key_pool, page_table, row_index).astype(jnp.float32)
        cached_values = gather_row(value_pool, page_table, row_index).astype(jnp.float32)
        scores = jnp.einsum('hgd,thd->hgt', query_row, cached_keys, precision=lax.Precision.HIGHEST) * score_scale
        live_mask = jnp.arange(MAXLEN, dtype=jnp.int32) < lengths[row_index]
        scores = jnp.where(live_mask[None, None, :], scores, jnp.float32(-1e+30))
        fresh_score = jnp.einsum('hgd,hd->hg', query_row, fresh_key, precision=lax.Precision.HIGHEST) * score_scale
        peak_score = jnp.maximum(lax.optimization_barrier(jnp.max(scores, axis=-1)), fresh_score)
        weights = jnp.exp(scores - peak_score[..., None]) * live_mask.astype(jnp.float32)[None, None, :]
        fresh_weight = jnp.exp(fresh_score - peak_score)
        weight_total = lax.optimization_barrier(jnp.sum(weights, axis=-1)) + fresh_weight
        rounded_weights = lax.optimization_barrier(weights.astype(jnp.bfloat16)).astype(jnp.float32)
        weighted = jnp.einsum('hgt,thd->hgd', rounded_weights, cached_values, precision=lax.Precision.HIGHEST)
        weighted = weighted + fresh_weight[..., None] * fresh_value[:, None, :]
        return (weighted / weight_total[..., None]).reshape(H * HD)
    attended = lax.map(attend, jnp.arange(ROWS, dtype=jnp.int32)).astype(jnp.bfloat16)
    projected = jnp.dot(attended, out_weight, preferred_element_type=jnp.float32)
    middle = (residual.astype(jnp.float32) + projected).astype(jnp.bfloat16)
    middle_f = middle.astype(jnp.float32)
    inverse = 1.0 / jnp.sqrt(lax.optimization_barrier(jnp.mean(middle_f * middle_f, axis=1)) + 1e-05)
    scaled = (middle_f * norm_gain.astype(jnp.float32)[None, :]).astype(jnp.bfloat16)
    gate = jnp.dot(scaled, gate_weight, preferred_element_type=jnp.float32) * inverse[:, None]
    up_part = jnp.dot(scaled, up_weight, preferred_element_type=jnp.float32) * inverse[:, None]
    hidden = (jax.nn.silu(gate) * up_part).astype(jnp.bfloat16)
    down = jnp.dot(hidden, down_weight, preferred_element_type=jnp.float32)
    return (middle_f + down).astype(jnp.bfloat16)
```

```python
import functools
import math

import jax
import jax.numpy as jnp
from jax import lax
from jax.experimental import pallas as pl
from jax.experimental.pallas import tpu as pltpu
from jax.sharding import PartitionSpec as P

D = 8192
KVH = 8
HD = 128
PAGE = 64
PMAX = 12
G = 8
ROWS_DEV = 2
SLOTS = ROWS_DEV * PMAX
TOKENS = SLOTS * PAGE
QROWS = ROWS_DEV * KVH * G
CHUNKS = 4
CHUNK = TOKENS // CHUNKS
NEG = -1e30
SHARD_AXES = ("ctx", "side")

norm_eps = 1e-05
f32 = jnp.float32
bf16 = jnp.bfloat16


def attend_kernel(
    table, lengths, q_ref, nk_ref, nv_ref, key_hbm, value_hbm, out_ref,
    keys, values, q_wide, scores, owner, key_sem, value_sem,
):
    shard = lax.axis_index(SHARD_AXES)

    def copy(src, dst, sem, c):
        rows = pl.ds(c * CHUNK, CHUNK)
        return pltpu.make_async_copy(src.at[rows], dst.at[rows], sem.at[c])

    for c in range(CHUNKS):
        copy(key_hbm, keys, key_sem, c).start()
    for c in range(CHUNKS):
        copy(value_hbm, values, value_sem, c).start()

    for k in range(SLOTS):
        owner[table[0, 0, k]] = k

    def limit_of(slot, row):
        k = owner[slot]
        own = lax.div(k, PMAX)
        page = lax.rem(k, PMAX)
        start = (page * 8 + shard) * PAGE
        count = lengths[row] - start
        return jnp.where(own == row, count, 0)

    q = q_ref[...]
    head_of_row = lax.rem(lax.div(lax.broadcasted_iota(jnp.int32, (QROWS, HD), 0), G), KVH)
    for h in range(KVH):
        q_wide[:, h * HD : (h + 1) * HD] = jnp.where(head_of_row == h, q, jnp.zeros_like(q))

    scale = 1.0 / math.sqrt(HD)

    def per_group(ref):
        parts = []
        for r in range(ROWS_DEV):
            for h in range(KVH):
                one = ref[r : r + 1, h * HD : (h + 1) * HD].astype(f32)
                parts.append(jnp.broadcast_to(one, (G, HD)))
        return jnp.concatenate(parts, axis=0)

    fresh = jnp.sum(q.astype(f32) * per_group(nk_ref), axis=1, keepdims=True) * scale
    fresh = jnp.where(shard == 0, fresh, NEG)
    new_values = per_group(nv_ref)

    lane = lax.broadcasted_iota(jnp.int32, (QROWS // ROWS_DEV, HD), 1)
    within = lax.rem(lane, PAGE)
    first_half = lane < PAGE
    peak = fresh
    for c in range(CHUNKS):
        copy(key_hbm, keys, key_sem, c).wait()
        part = lax.dot_general(
            q_wide[...], keys[c * CHUNK : (c + 1) * CHUNK, :],
            (((1,), (1,)), ((), ())), preferred_element_type=f32,
        ) * scale
        for t in range(CHUNK // HD):
            slot = (c * CHUNK + t * HD) // PAGE
            tiles = []
            for r in range(ROWS_DEV):
                live = within < jnp.where(first_half, limit_of(slot, r), limit_of(slot + 1, r))
                tile = part[r * KVH * G : (r + 1) * KVH * G, t * HD : (t + 1) * HD]
                tiles.append(jnp.where(live, tile, NEG))
            tile = jnp.concatenate(tiles, axis=0)
            scores[:, c * CHUNK + t * HD : c * CHUNK + (t + 1) * HD] = tile
            peak = jnp.maximum(peak, jnp.max(tile, axis=1, keepdims=True))

    total = jnp.zeros((QROWS, HD), f32)
    mixed = jnp.zeros((QROWS, KVH * HD), f32)
    for c in range(CHUNKS):
        part = scores[:, c * CHUNK : (c + 1) * CHUNK]
        weight = jnp.where(part > 0.5 * NEG, jnp.exp(part - peak), 0.0)
        for t in range(CHUNK // HD):
            total = total + weight[:, t * HD : (t + 1) * HD]
        copy(value_hbm, values, value_sem, c).wait()
        mixed = mixed + jnp.dot(
            weight.astype(bf16), values[c * CHUNK : (c + 1) * CHUNK, :], preferred_element_type=f32
        )
    fresh_weight = jnp.where(shard == 0, jnp.exp(fresh - peak), 0.0)
    total = jnp.sum(total, axis=1, keepdims=True) + fresh_weight
    added = fresh_weight * new_values
    stat_lane = lax.broadcasted_iota(jnp.int32, (QROWS, HD), 1)
    stats = jnp.where(stat_lane == 0, peak, total)
    for h in range(KVH):
        for r in range(ROWS_DEV):
            at = (r * KVH + h) * G
            own = mixed[at : at + G, h * HD : (h + 1) * HD] + added[at : at + G, :]
            out_ref[h, r * G : (r + 1) * G, 0:HD] = own
            out_ref[h, r * G : (r + 1) * G, HD : 2 * HD] = stats[at : at + G, :]


def attend(table, lengths, q, new_key, new_value, keys, values):
    smem = pl.BlockSpec(memory_space=pltpu.SMEM)
    vmem = pl.BlockSpec(memory_space=pltpu.VMEM)
    hbm = pl.BlockSpec(memory_space=pl.ANY)
    return pl.pallas_call(
        attend_kernel,
        out_shape=jax.ShapeDtypeStruct((KVH, ROWS_DEV * G, 2 * HD), f32),
        in_specs=[smem, smem, vmem, vmem, vmem, hbm, hbm],
        out_specs=vmem,
        scratch_shapes=[
            pltpu.VMEM((TOKENS, KVH * HD), bf16),
            pltpu.VMEM((TOKENS, KVH * HD), bf16),
            pltpu.VMEM((QROWS, KVH * HD), bf16),
            pltpu.VMEM((QROWS, TOKENS), f32),
            pltpu.SMEM((SLOTS,), jnp.int32),
            pltpu.SemaphoreType.DMA((CHUNKS,)),
            pltpu.SemaphoreType.DMA((CHUNKS,)),
        ],
        compiler_params=pltpu.CompilerParams(vmem_limit_bytes=24 * 1024 * 1024),
        name="attend",
    )(table, lengths, q, new_key, new_value, keys, values)


def merge_kernel(parts_ref, out_ref, wide):
    shards = parts_ref.shape[0]
    peak = parts_ref[0, :, HD : HD + 1]
    for s in range(1, shards):
        peak = jnp.maximum(peak, parts_ref[s, :, HD : HD + 1])
    total = jnp.zeros_like(peak)
    mixed = jnp.zeros((ROWS_DEV * G, HD), f32)
    for s in range(shards):
        factor = jnp.exp(parts_ref[s, :, HD : HD + 1] - peak)
        total = total + factor * parts_ref[s, :, HD + 1 : HD + 2]
        mixed = mixed + factor * parts_ref[s, :, 0:HD]
    attended = mixed / total
    for r in range(ROWS_DEV):
        for g in range(G):
            wide[r : r + 1, g * HD : (g + 1) * HD] = attended[r * G + g : r * G + g + 1, :]
    out_ref[...] = wide[0:ROWS_DEV, :].astype(bf16)


def merge(parts):
    vmem = pl.BlockSpec(memory_space=pltpu.VMEM)
    return pl.pallas_call(
        merge_kernel,
        out_shape=jax.ShapeDtypeStruct((ROWS_DEV, G * HD), bf16),
        in_specs=[vmem],
        out_specs=vmem,
        scratch_shapes=[pltpu.VMEM((8, G * HD), f32)],
        name="merge",
    )(parts)


def gather(x, axes):
    copies = jnp.broadcast_to(x[None], (lax.axis_size(axes),) + x.shape)
    return lax.all_to_all(copies, axes, 0, 0)


def body(
    queries,
    new_key,
    new_value,
    key_pool,
    value_pool,
    page_table,
    lengths,
    residual,
    out_weight,
    norm_gain,
    gate_weight,
    up_weight,
    down_weight,
):
    shards = lax.axis_size(SHARD_AXES)
    groups = lax.axis_size("dp")
    shard_index = lax.axis_index(SHARD_AXES)
    rows = residual.shape[0]
    hidden_here = gate_weight.shape[1]

    parts = attend(
        page_table,
        lengths,
        queries.reshape(QROWS, HD),
        new_key,
        new_value,
        key_pool.reshape(TOKENS, KVH * HD),
        value_pool.reshape(TOKENS, KVH * HD),
    )
    attended = merge(lax.all_to_all(parts, SHARD_AXES, 0, 0))
    attended = gather(attended, "dp").reshape(rows, G * HD)
    partial_proj = jnp.dot(attended, out_weight, preferred_element_type=f32).astype(bf16)
    projected = jnp.sum(gather(partial_proj, SHARD_AXES).astype(f32), axis=0)
    middle = (residual.astype(f32) + projected).astype(bf16)
    middle_f = middle.astype(f32)
    scaled = (middle_f * norm_gain[None, :]).astype(bf16)
    squares = jnp.sum(middle_f * middle_f, axis=1, keepdims=True)
    squares_high = squares.astype(bf16)
    squares_low = (squares - squares_high.astype(f32)).astype(bf16)
    gate_part = jnp.dot(scaled, gate_weight, preferred_element_type=f32).astype(bf16)
    up_part = jnp.dot(scaled, up_weight, preferred_element_type=f32).astype(bf16)
    pad = jnp.zeros((rows, HD - 2), bf16)
    sent = jnp.concatenate([gate_part, up_part, squares_high, squares_low, pad], axis=1)
    came = lax.all_to_all(
        sent.reshape(groups, ROWS_DEV, sent.shape[1]), "dp", 0, 0
    )
    sums = jnp.sum(came.astype(f32), axis=0)
    square_sum = sums[:, 2 * hidden_here] + sums[:, 2 * hidden_here + 1]
    inverse = (1.0 / jnp.sqrt(square_sum / D + norm_eps))[:, None]
    gate = sums[:, :hidden_here] * inverse
    up = sums[:, hidden_here : 2 * hidden_here] * inverse
    hidden = (jax.nn.silu(gate) * up).astype(bf16)
    hidden = gather(hidden, "dp").reshape(rows, hidden_here)
    down = jnp.dot(hidden, down_weight, preferred_element_type=f32)
    share_rows = rows // shards
    down = lax.all_to_all(down.reshape(shards, share_rows, down.shape[1]), SHARD_AXES, 0, 0)
    middle_own = lax.dynamic_slice_in_dim(middle_f, shard_index * share_rows, share_rows, 0)
    return (middle_own + jnp.sum(down, axis=0)).astype(bf16)


def solution(mesh):
    placed = (
        P("dp", None),
        P("dp", None),
        P("dp", None),
        P(("dp", "ctx", "side"), None, None),
        P(("dp", "ctx", "side"), None, None),
        P("dp", ("ctx", "side"), None),
        P("dp"),
        P(None, "dp"),
        P(("ctx", "side"), "dp"),
        P("dp"),
        P("dp", ("ctx", "side")),
        P("dp", ("ctx", "side")),
        P(("ctx", "side"), "dp"),
    )
    return jax.shard_map(
        body, mesh=mesh, in_specs=placed, out_specs=P(("ctx", "side"), "dp"), check_vma=False
    )
```

```python
import math

import jax
import jax.numpy as jnp
from jax import lax
from jax.experimental import pallas as pl
from jax.experimental.pallas import tpu as pltpu
from jax.sharding import Mesh
from jax.sharding import PartitionSpec as P

D = 8192
KVH = 8
HD = 128
PAGE = 64
PMAX = 12
G = 8
ROWS_DEV = 2
SLOTS = ROWS_DEV * PMAX
TOKENS = SLOTS * PAGE
QROWS = ROWS_DEV * KVH * G
CHUNKS = 4
CHUNK = TOKENS // CHUNKS
NEG = -1e30
SHARD_AXES = ("ctx", "side")
DP_AXES = ("z2", "z1", "z0", "y1", "y0")
SUM_AXES = ("y1", "y0", "z2", "z1", "z0")
WIDE_STEPS = 7
ATTEND_VMEM = 64 * 1024 * 1024

norm_eps = 1e-05
f32 = jnp.float32
bf16 = jnp.bfloat16


def attend_kernel(
    table_hbm, lengths_hbm, q_hbm, nk_hbm, nv_hbm, key_hbm, value_hbm, out_ref,
    table, lengths, q_two, nk_ref, nv_ref, q_rows, keys, values, q_wide, scores, owner,
    small_sem, key_sem, value_sem,
):
    shard = lax.axis_index(SHARD_AXES)
    small = [
        pltpu.make_async_copy(src, dst, small_sem.at[i])
        for i, (src, dst) in enumerate(
            [(q_hbm, q_two), (nk_hbm, nk_ref), (nv_hbm, nv_ref), (table_hbm, table), (lengths_hbm, lengths)]
        )
    ]
    for one in small:
        one.start()

    def copy(src, dst, sem, c):
        rows = pl.ds(c * CHUNK, CHUNK)
        return pltpu.make_async_copy(src.at[rows], dst.at[rows], sem.at[c])

    for c in range(CHUNKS):
        copy(key_hbm, keys, key_sem, c).start()
    for c in range(CHUNKS):
        copy(value_hbm, values, value_sem, c).start()

    for one in small:
        one.wait()

    for k in range(SLOTS):
        owner[table[0, 0, k]] = k

    def limit_of(slot, row):
        k = owner[slot]
        own = lax.div(k, PMAX)
        page = lax.rem(k, PMAX)
        start = (page * 8 + shard) * PAGE
        count = lengths[row] - start
        return jnp.where(own == row, count, 0)

    q_all = q_two[...].astype(f32)
    for n in range(KVH * G):
        for r in range(ROWS_DEV):
            at = r * KVH * G + n
            q_rows[at : at + 1, :] = q_all[r : r + 1, n * HD : (n + 1) * HD]
    q = q_rows[...].astype(bf16)
    head_of_row = lax.rem(lax.div(lax.broadcasted_iota(jnp.int32, (QROWS, HD), 0), G), KVH)
    for h in range(KVH):
        q_wide[:, h * HD : (h + 1) * HD] = jnp.where(head_of_row == h, q, jnp.zeros_like(q))

    scale = 1.0 / math.sqrt(HD)

    def per_group(ref):
        parts = []
        for r in range(ROWS_DEV):
            for h in range(KVH):
                one = ref[r : r + 1, h * HD : (h + 1) * HD].astype(f32)
                parts.append(jnp.broadcast_to(one, (G, HD)))
        return jnp.concatenate(parts, axis=0)

    fresh = jnp.sum(q.astype(f32) * per_group(nk_ref), axis=1, keepdims=True) * scale
    fresh = jnp.where(shard == 0, fresh, NEG)
    new_values = per_group(nv_ref)

    lane = lax.broadcasted_iota(jnp.int32, (QROWS // ROWS_DEV, HD), 1)
    within = lax.rem(lane, PAGE)
    first_half = lane < PAGE
    peak = fresh
    for c in range(CHUNKS):
        copy(key_hbm, keys, key_sem, c).wait()
        part = lax.dot_general(
            q_wide[...], keys[c * CHUNK : (c + 1) * CHUNK, :],
            (((1,), (1,)), ((), ())), preferred_element_type=f32,
        ) * scale
        for t in range(CHUNK // HD):
            slot = (c * CHUNK + t * HD) // PAGE
            tiles = []
            for r in range(ROWS_DEV):
                live = within < jnp.where(first_half, limit_of(slot, r), limit_of(slot + 1, r))
                tile = part[r * KVH * G : (r + 1) * KVH * G, t * HD : (t + 1) * HD]
                tiles.append(jnp.where(live, tile, NEG))
            tile = jnp.concatenate(tiles, axis=0)
            scores[:, c * CHUNK + t * HD : c * CHUNK + (t + 1) * HD] = tile
            peak = jnp.maximum(peak, jnp.max(tile, axis=1, keepdims=True))

    total = jnp.zeros((QROWS, HD), f32)
    mixed = jnp.zeros((QROWS, KVH * HD), f32)
    for c in range(CHUNKS):
        part = scores[:, c * CHUNK : (c + 1) * CHUNK]
        weight = jnp.where(part > 0.5 * NEG, jnp.exp(part - peak), 0.0)
        for t in range(CHUNK // HD):
            total = total + weight[:, t * HD : (t + 1) * HD]
        copy(value_hbm, values, value_sem, c).wait()
        mixed = mixed + jnp.dot(
            weight.astype(bf16), values[c * CHUNK : (c + 1) * CHUNK, :], preferred_element_type=f32
        )
    fresh_weight = jnp.where(shard == 0, jnp.exp(fresh - peak), 0.0)
    total = jnp.sum(total, axis=1, keepdims=True) + fresh_weight
    added = fresh_weight * new_values
    stat_lane = lax.broadcasted_iota(jnp.int32, (QROWS, HD), 1)
    stats = jnp.where(stat_lane == 0, peak, total)
    for h in range(KVH):
        for r in range(ROWS_DEV):
            at = (r * KVH + h) * G
            own = mixed[at : at + G, h * HD : (h + 1) * HD] + added[at : at + G, :]
            out_ref[h, r * G : (r + 1) * G, 0:HD] = own
            out_ref[h, r * G : (r + 1) * G, HD : 2 * HD] = stats[at : at + G, :]


def attend(table, lengths, q, new_key, new_value, keys, values):
    vmem = pl.BlockSpec(memory_space=pltpu.VMEM)
    hbm = pl.BlockSpec(memory_space=pltpu.HBM)
    return pl.pallas_call(
        attend_kernel,
        out_shape=jax.ShapeDtypeStruct((KVH, ROWS_DEV * G, 2 * HD), f32),
        in_specs=[hbm] * 7,
        out_specs=vmem,
        scratch_shapes=[
            pltpu.SMEM((1, 1, SLOTS), jnp.int32),
            pltpu.SMEM((ROWS_DEV,), jnp.int32),
            pltpu.VMEM((ROWS_DEV, KVH * G * HD), bf16),
            pltpu.VMEM((ROWS_DEV, KVH * HD), bf16),
            pltpu.VMEM((ROWS_DEV, KVH * HD), bf16),
            pltpu.VMEM((QROWS, HD), f32),
            pltpu.VMEM((TOKENS, KVH * HD), bf16),
            pltpu.VMEM((TOKENS, KVH * HD), bf16),
            pltpu.VMEM((QROWS, KVH * HD), bf16),
            pltpu.VMEM((QROWS, TOKENS), f32),
            pltpu.SMEM((SLOTS,), jnp.int32),
            pltpu.SemaphoreType.DMA((5,)),
            pltpu.SemaphoreType.DMA((CHUNKS,)),
            pltpu.SemaphoreType.DMA((CHUNKS,)),
        ],
        compiler_params=pltpu.CompilerParams(vmem_limit_bytes=ATTEND_VMEM),
        name="attend",
    )(table, lengths, q, new_key, new_value, keys, values)


def merge_kernel(parts_ref, out_ref):
    shards = parts_ref.shape[0]
    peak = parts_ref[0, :, HD : HD + 1]
    for s in range(1, shards):
        peak = jnp.maximum(peak, parts_ref[s, :, HD : HD + 1])
    total = jnp.zeros_like(peak)
    mixed = jnp.zeros((ROWS_DEV * G, HD), f32)
    for s in range(shards):
        factor = jnp.exp(parts_ref[s, :, HD : HD + 1] - peak)
        total = total + factor * parts_ref[s, :, HD + 1 : HD + 2]
        mixed = mixed + factor * parts_ref[s, :, 0:HD]
    attended = (mixed / total).astype(bf16)
    for i in range(out_ref.shape[0]):
        out_ref[i] = attended


def merge(parts, copies):
    vmem = pl.BlockSpec(memory_space=pltpu.VMEM)
    return pl.pallas_call(
        merge_kernel,
        out_shape=jax.ShapeDtypeStruct((copies, ROWS_DEV * G, HD), bf16),
        in_specs=[vmem],
        out_specs=vmem,
        compiler_params=pltpu.CompilerParams(vmem_limit_bytes=4 * 1024 * 1024),
        cost_estimate=pl.CostEstimate(flops=20_000_000_000, bytes_accessed=0, transcendentals=0),
        name="merge",
    )(parts)


def project_kernel(attended_ref, weight_ref, out_ref, rows_ref):
    groups = attended_ref.shape[0]
    for n in range(groups):
        rows_ref[n * ROWS_DEV * G : (n + 1) * ROWS_DEV * G, :] = attended_ref[n].astype(f32)
    heads = [rows_ref[pl.ds(g, groups * ROWS_DEV, stride=G), :] for g in range(G)]
    wide = jnp.concatenate(heads, axis=1).astype(bf16)
    result = jnp.dot(wide, weight_ref[...], preferred_element_type=f32).astype(bf16)
    for i in range(out_ref.shape[0]):
        out_ref[i] = result


def project(attended, weight, copies):
    groups = attended.shape[0]
    vmem = pl.BlockSpec(memory_space=pltpu.VMEM)
    return pl.pallas_call(
        project_kernel,
        out_shape=jax.ShapeDtypeStruct((copies, groups * ROWS_DEV, weight.shape[1]), bf16),
        in_specs=[vmem, vmem],
        out_specs=vmem,
        scratch_shapes=[pltpu.VMEM((groups * ROWS_DEV * G, HD), f32)],
        compiler_params=pltpu.CompilerParams(vmem_limit_bytes=8 * 1024 * 1024),
        cost_estimate=pl.CostEstimate(flops=20_000_000_000, bytes_accessed=0, transcendentals=0),
        name="project",
    )(attended, weight)


def widen_kernel(came_ref, residual_ref, gain_ref, gate_ref, up_ref, sent_ref, middle_ref):
    hidden_here = gate_ref.shape[1]
    step = hidden_here // WIDE_STEPS
    projected = came_ref[0].astype(f32)
    for s in range(1, came_ref.shape[0]):
        projected = projected + came_ref[s].astype(f32)
    middle = (residual_ref[...].astype(f32) + projected).astype(bf16)
    middle_ref[...] = middle
    middle_f = middle.astype(f32)
    scaled = (middle_f * gain_ref[...]).astype(bf16)
    squares = jnp.sum(middle_f * middle_f, axis=1, keepdims=True)
    high = squares.astype(bf16).astype(f32)
    lane = lax.broadcasted_iota(jnp.int32, (middle.shape[0], HD), 1)
    tail = jnp.where(lane == 0, high, jnp.where(lane == 1, squares - high, 0.0))
    sent_ref[:, 2 * hidden_here :] = tail.astype(bf16)
    for n, weight_ref in enumerate((gate_ref, up_ref)):
        for c in range(WIDE_STEPS):
            at = n * hidden_here + c * step
            sent_ref[:, at : at + step] = jnp.dot(
                scaled, weight_ref[:, c * step : (c + 1) * step], preferred_element_type=f32
            ).astype(bf16)


def widen(came, residual, gain, gate_weight, up_weight):
    rows, width = residual.shape
    hidden_here = gate_weight.shape[1]
    vmem = pl.BlockSpec(memory_space=pltpu.VMEM)
    return pl.pallas_call(
        widen_kernel,
        out_shape=(
            jax.ShapeDtypeStruct((rows, 2 * hidden_here + HD), bf16),
            jax.ShapeDtypeStruct((rows, width), bf16),
        ),
        in_specs=[vmem] * 5,
        out_specs=(vmem, vmem),
        compiler_params=pltpu.CompilerParams(vmem_limit_bytes=8 * 1024 * 1024),
        name="widen",
    )(came, residual, gain, gate_weight, up_weight)


def narrow_kernel(hidden_ref, down_ref, out_ref):
    out_ref[...] = jnp.dot(hidden_ref[...], down_ref[...], preferred_element_type=f32)


def narrow(hidden, down_weight):
    vmem = pl.BlockSpec(memory_space=pltpu.VMEM)
    return pl.pallas_call(
        narrow_kernel,
        out_shape=jax.ShapeDtypeStruct((hidden.shape[0], down_weight.shape[1]), f32),
        in_specs=[vmem, vmem],
        out_specs=vmem,
        compiler_params=pltpu.CompilerParams(vmem_limit_bytes=8 * 1024 * 1024),
        name="narrow",
    )(hidden, down_weight)


def copies_for(x, axes):
    return jnp.broadcast_to(x[None], (lax.axis_size(axes),) + x.shape)


def body(
    queries,
    new_key,
    new_value,
    key_pool,
    value_pool,
    page_table,
    lengths,
    residual,
    out_weight,
    norm_gain,
    gate_weight,
    up_weight,
    down_weight,
):
    shards = lax.axis_size(SHARD_AXES)
    shard_index = lax.axis_index(SHARD_AXES)
    rows, width = residual.shape
    hidden_here = gate_weight.shape[1]

    parts = attend(
        page_table,
        lengths,
        queries,
        new_key,
        new_value,
        key_pool.reshape(TOKENS, KVH * HD),
        value_pool.reshape(TOKENS, KVH * HD),
    )
    attended = merge(lax.all_to_all(parts, SHARD_AXES, 0, 0), lax.axis_size(DP_AXES))
    attended = lax.all_to_all(attended, DP_AXES, 0, 0)
    partial_proj = project(attended, out_weight, shards)
    came = lax.all_to_all(partial_proj, SHARD_AXES, 0, 0)
    sent, middle = widen(came, residual, norm_gain.reshape(1, width), gate_weight, up_weight)
    near, far = SUM_AXES[:2], SUM_AXES[2:]
    spread = lax.axis_size(near)
    came = lax.all_to_all(sent.reshape(spread, rows // spread, sent.shape[1]), near, 0, 0)
    sent = jnp.sum(came.astype(f32), axis=0).astype(bf16)
    came = lax.all_to_all(sent.reshape(lax.axis_size(far), ROWS_DEV, sent.shape[1]), far, 0, 0)
    sums = jnp.sum(came.astype(f32), axis=0)
    square_sum = sums[:, 2 * hidden_here] + sums[:, 2 * hidden_here + 1]
    inverse = (1.0 / jnp.sqrt(square_sum / D + norm_eps))[:, None]
    gate = sums[:, :hidden_here] * inverse
    up = sums[:, hidden_here : 2 * hidden_here] * inverse
    hidden = (jax.nn.silu(gate) * up).astype(bf16)
    hidden = lax.all_to_all(copies_for(hidden, SUM_AXES), SUM_AXES, 0, 0)
    down = narrow(hidden.reshape(rows, hidden_here), down_weight)
    share_rows = rows // shards
    down = lax.all_to_all(down.reshape(shards, share_rows, width), SHARD_AXES, 0, 0)
    middle_own = lax.dynamic_slice_in_dim(middle, shard_index * share_rows, share_rows, 0)
    return (middle_own.astype(f32) + jnp.sum(down, axis=0)).astype(bf16)


def solution(mesh):
    lines, cores = mesh.shape["ctx"], mesh.shape["side"]
    split = Mesh(
        mesh.devices.reshape((2,) * len(DP_AXES) + (lines, cores)), DP_AXES + SHARD_AXES
    )
    dp, block = DP_AXES, SHARD_AXES
    placed = (
        P(dp, None),
        P(dp, None),
        P(dp, None),
        P(dp + block, None, None),
        P(dp + block, None, None),
        P(dp, block, None),
        P(dp),
        P(None, dp),
        P(block, dp),
        P(dp),
        P(dp, block),
        P(dp, block),
        P(block, dp),
    )
    return jax.shard_map(
        body, mesh=split, in_specs=placed, out_specs=P(block, dp), check_vma=False
    )
```

```python
import math

import jax
import jax.numpy as jnp
from jax import lax
from jax.experimental import pallas as pl
from jax.experimental.pallas import tpu as pltpu
from jax.sharding import Mesh
from jax.sharding import PartitionSpec as P

D = 8192
KVH = 8
HD = 128
PAGE = 64
PMAX = 12
G = 8
ROWS_DEV = 2
SLOTS = ROWS_DEV * PMAX
TOKENS = SLOTS * PAGE
QROWS = ROWS_DEV * KVH * G
CHUNKS = 4
CHUNK = TOKENS // CHUNKS
NEG = -1e30
SHARD_AXES = ("ctx", "side")
DP_AXES = ("z2", "z1", "z0", "y1", "y0")
NEAR_AXES = ("y1", "y0", "z0")
FAR_AXES = ("z2", "z1")
SPREAD_Y = 4
ATTEND_VMEM = 64 * 1024 * 1024

norm_eps = 1e-05
f32 = jnp.float32
bf16 = jnp.bfloat16


def attend_kernel(
    table_hbm, lengths_hbm, q_hbm, nk_hbm, nv_hbm, key_hbm, value_hbm, out_ref,
    table, lengths, q_two, nk_ref, nv_ref, q_rows, keys, values, q_wide, scores, owner,
    small_sem, key_sem, value_sem,
):
    shard = lax.axis_index(SHARD_AXES)
    small = [
        pltpu.make_async_copy(src, dst, small_sem.at[i])
        for i, (src, dst) in enumerate(
            [(q_hbm, q_two), (nk_hbm, nk_ref), (nv_hbm, nv_ref), (table_hbm, table), (lengths_hbm, lengths)]
        )
    ]
    for one in small:
        one.start()

    def copy(src, dst, sem, c):
        rows = pl.ds(c * CHUNK, CHUNK)
        return pltpu.make_async_copy(src.at[rows], dst.at[rows], sem.at[c])

    for c in range(CHUNKS):
        copy(key_hbm, keys, key_sem, c).start()
    for c in range(CHUNKS):
        copy(value_hbm, values, value_sem, c).start()

    for one in small:
        one.wait()

    for k in range(SLOTS):
        owner[table[0, 0, k]] = k

    def limit_of(slot, row):
        k = owner[slot]
        own = lax.div(k, PMAX)
        page = lax.rem(k, PMAX)
        start = (page * 8 + shard) * PAGE
        count = lengths[row] - start
        return jnp.where(own == row, count, 0)

    q_all = q_two[...].astype(f32)
    for n in range(KVH * G):
        for r in range(ROWS_DEV):
            at = r * KVH * G + n
            q_rows[at : at + 1, :] = q_all[r : r + 1, n * HD : (n + 1) * HD]
    q = q_rows[...].astype(bf16)
    head_of_row = lax.rem(lax.div(lax.broadcasted_iota(jnp.int32, (QROWS, HD), 0), G), KVH)
    for h in range(KVH):
        q_wide[:, h * HD : (h + 1) * HD] = jnp.where(head_of_row == h, q, jnp.zeros_like(q))

    scale = 1.0 / math.sqrt(HD)

    def per_group(ref):
        parts = []
        for r in range(ROWS_DEV):
            for h in range(KVH):
                one = ref[r : r + 1, h * HD : (h + 1) * HD].astype(f32)
                parts.append(jnp.broadcast_to(one, (G, HD)))
        return jnp.concatenate(parts, axis=0)

    fresh = jnp.sum(q.astype(f32) * per_group(nk_ref), axis=1, keepdims=True) * scale
    fresh = jnp.where(shard == 0, fresh, NEG)
    new_values = per_group(nv_ref)

    lane = lax.broadcasted_iota(jnp.int32, (QROWS // ROWS_DEV, HD), 1)
    within = lax.rem(lane, PAGE)
    first_half = lane < PAGE
    peak = fresh
    for c in range(CHUNKS):
        copy(key_hbm, keys, key_sem, c).wait()
        part = lax.dot_general(
            q_wide[...], keys[c * CHUNK : (c + 1) * CHUNK, :],
            (((1,), (1,)), ((), ())), preferred_element_type=f32,
        ) * scale
        for t in range(CHUNK // HD):
            slot = (c * CHUNK + t * HD) // PAGE
            tiles = []
            for r in range(ROWS_DEV):
                live = within < jnp.where(first_half, limit_of(slot, r), limit_of(slot + 1, r))
                tile = part[r * KVH * G : (r + 1) * KVH * G, t * HD : (t + 1) * HD]
                tiles.append(jnp.where(live, tile, NEG))
            tile = jnp.concatenate(tiles, axis=0)
            scores[:, c * CHUNK + t * HD : c * CHUNK + (t + 1) * HD] = tile
            peak = jnp.maximum(peak, jnp.max(tile, axis=1, keepdims=True))

    total = jnp.zeros((QROWS, HD), f32)
    mixed = jnp.zeros((QROWS, KVH * HD), f32)
    for c in range(CHUNKS):
        part = scores[:, c * CHUNK : (c + 1) * CHUNK]
        weight = jnp.where(part > 0.5 * NEG, jnp.exp(part - peak), 0.0)
        for t in range(CHUNK // HD):
            total = total + weight[:, t * HD : (t + 1) * HD]
        copy(value_hbm, values, value_sem, c).wait()
        mixed = mixed + jnp.dot(
            weight.astype(bf16), values[c * CHUNK : (c + 1) * CHUNK, :], preferred_element_type=f32
        )
    fresh_weight = jnp.where(shard == 0, jnp.exp(fresh - peak), 0.0)
    total = jnp.sum(total, axis=1, keepdims=True) + fresh_weight
    added = fresh_weight * new_values
    stat_lane = lax.broadcasted_iota(jnp.int32, (QROWS, HD), 1)
    stats = jnp.where(stat_lane == 0, peak, total)
    for h in range(KVH):
        for r in range(ROWS_DEV):
            at = (r * KVH + h) * G
            own = mixed[at : at + G, h * HD : (h + 1) * HD] + added[at : at + G, :]
            out_ref[h, r * G : (r + 1) * G, 0:HD] = own
            out_ref[h, r * G : (r + 1) * G, HD : 2 * HD] = stats[at : at + G, :]


def attend(table, lengths, q, new_key, new_value, keys, values):
    vmem = pl.BlockSpec(memory_space=pltpu.VMEM)
    hbm = pl.BlockSpec(memory_space=pltpu.HBM)
    return pl.pallas_call(
        attend_kernel,
        out_shape=jax.ShapeDtypeStruct((KVH, ROWS_DEV * G, 2 * HD), f32),
        in_specs=[hbm] * 7,
        out_specs=vmem,
        scratch_shapes=[
            pltpu.SMEM((1, 1, SLOTS), jnp.int32),
            pltpu.SMEM((ROWS_DEV,), jnp.int32),
            pltpu.VMEM((ROWS_DEV, KVH * G * HD), bf16),
            pltpu.VMEM((ROWS_DEV, KVH * HD), bf16),
            pltpu.VMEM((ROWS_DEV, KVH * HD), bf16),
            pltpu.VMEM((QROWS, HD), f32),
            pltpu.VMEM((TOKENS, KVH * HD), bf16),
            pltpu.VMEM((TOKENS, KVH * HD), bf16),
            pltpu.VMEM((QROWS, KVH * HD), bf16),
            pltpu.VMEM((QROWS, TOKENS), f32),
            pltpu.SMEM((SLOTS,), jnp.int32),
            pltpu.SemaphoreType.DMA((5,)),
            pltpu.SemaphoreType.DMA((CHUNKS,)),
            pltpu.SemaphoreType.DMA((CHUNKS,)),
        ],
        compiler_params=pltpu.CompilerParams(vmem_limit_bytes=ATTEND_VMEM),
        name="attend",
    )(table, lengths, q, new_key, new_value, keys, values)


def merge_kernel(parts_ref, out_ref):
    shards = parts_ref.shape[0]
    peak = parts_ref[0, :, HD : HD + 1]
    for s in range(1, shards):
        peak = jnp.maximum(peak, parts_ref[s, :, HD : HD + 1])
    total = jnp.zeros_like(peak)
    mixed = jnp.zeros((ROWS_DEV * G, HD), f32)
    for s in range(shards):
        factor = jnp.exp(parts_ref[s, :, HD : HD + 1] - peak)
        total = total + factor * parts_ref[s, :, HD + 1 : HD + 2]
        mixed = mixed + factor * parts_ref[s, :, 0:HD]
    attended = (mixed / total).astype(bf16)
    for i in range(out_ref.shape[0]):
        out_ref[i] = attended


def merge(parts, copies):
    vmem = pl.BlockSpec(memory_space=pltpu.VMEM)
    return pl.pallas_call(
        merge_kernel,
        out_shape=jax.ShapeDtypeStruct((copies, ROWS_DEV * G, HD), bf16),
        in_specs=[vmem],
        out_specs=vmem,
        compiler_params=pltpu.CompilerParams(vmem_limit_bytes=4 * 1024 * 1024),
        cost_estimate=pl.CostEstimate(flops=20_000_000_000, bytes_accessed=0, transcendentals=0),
        name="merge",
    )(parts)


def project_kernel(attended_ref, weight_ref, out_ref, rows_ref):
    groups = attended_ref.shape[0]
    for n in range(groups):
        rows_ref[n * ROWS_DEV * G : (n + 1) * ROWS_DEV * G, :] = attended_ref[n].astype(f32)
    heads = [rows_ref[pl.ds(g, groups * ROWS_DEV, stride=G), :] for g in range(G)]
    wide = jnp.concatenate(heads, axis=1).astype(bf16)
    result = jnp.dot(wide, weight_ref[...], preferred_element_type=f32).astype(bf16)
    for i in range(out_ref.shape[0]):
        out_ref[i] = result


def project(attended, weight, copies):
    groups = attended.shape[0]
    vmem = pl.BlockSpec(memory_space=pltpu.VMEM)
    return pl.pallas_call(
        project_kernel,
        out_shape=jax.ShapeDtypeStruct((copies, groups * ROWS_DEV, weight.shape[1]), bf16),
        in_specs=[vmem, vmem],
        out_specs=vmem,
        scratch_shapes=[pltpu.VMEM((groups * ROWS_DEV * G, HD), f32)],
        compiler_params=pltpu.CompilerParams(vmem_limit_bytes=8 * 1024 * 1024),
        cost_estimate=pl.CostEstimate(flops=20_000_000_000, bytes_accessed=0, transcendentals=0),
        name="project",
    )(attended, weight)


def widen_kernel(
    came_ref, residual_ref, gain_ref, gate_ref, up_ref, sent_ref, own_ref, middle_ref
):
    projected = came_ref[0].astype(f32)
    for s in range(1, came_ref.shape[0]):
        projected = projected + came_ref[s].astype(f32)
    middle = (residual_ref[...].astype(f32) + projected).astype(bf16).astype(f32)
    middle_ref[...] = middle
    share = own_ref.shape[0]
    at = pl.multiple_of(lax.axis_index(SHARD_AXES) * share, share)
    own_ref[...] = middle_ref[pl.ds(at, share), :]
    scaled = (middle * gain_ref[...]).astype(bf16)
    squares = jnp.sum(middle * middle, axis=1, keepdims=True)
    high = squares.astype(bf16).astype(f32)
    lane = lax.broadcasted_iota(jnp.int32, (middle.shape[0], HD), 1)
    tail = jnp.where(lane == 0, high, jnp.where(lane == 1, squares - high, 0.0)).astype(bf16)
    blocks = sent_ref.shape[0]
    units = gate_ref.shape[1] // blocks
    for b in range(blocks):
        for n, weight_ref in enumerate((gate_ref, up_ref)):
            sent_ref[b, :, n * units : (n + 1) * units] = jnp.dot(
                scaled, weight_ref[:, b * units : (b + 1) * units], preferred_element_type=f32
            ).astype(bf16)
        sent_ref[b, :, 2 * units :] = tail


def widen(came, residual, gain, gate_weight, up_weight, blocks, share):
    rows, width = residual.shape
    units = gate_weight.shape[1] // blocks
    vmem = pl.BlockSpec(memory_space=pltpu.VMEM)
    return pl.pallas_call(
        widen_kernel,
        out_shape=(
            jax.ShapeDtypeStruct((blocks, rows, 2 * units + HD), bf16),
            jax.ShapeDtypeStruct((share, width), f32),
        ),
        in_specs=[vmem] * 5,
        out_specs=(vmem, vmem),
        scratch_shapes=[pltpu.VMEM((rows, width), f32)],
        compiler_params=pltpu.CompilerParams(vmem_limit_bytes=8 * 1024 * 1024),
        name="widen",
    )(came, residual, gain, gate_weight, up_weight)


def finish_kernel(came_ref, out_ref):
    units = out_ref.shape[2]
    sums = came_ref[0].astype(f32)
    for n in range(1, came_ref.shape[0]):
        sums = sums + came_ref[n].astype(f32)
    squares = sums[:, 2 * units : 2 * units + 1] + sums[:, 2 * units + 1 : 2 * units + 2]
    inverse = 1.0 / jnp.sqrt(squares / D + norm_eps)
    gate = sums[:, :units] * inverse
    up = sums[:, units : 2 * units] * inverse
    hidden = (gate / (1.0 + jnp.exp(-gate)) * up).astype(bf16)
    for n in range(out_ref.shape[0]):
        out_ref[n] = hidden


def finish(came, copies):
    _, rows, wide = came.shape
    vmem = pl.BlockSpec(memory_space=pltpu.VMEM)
    return pl.pallas_call(
        finish_kernel,
        out_shape=jax.ShapeDtypeStruct((copies, rows, (wide - HD) // 2), bf16),
        in_specs=[vmem],
        out_specs=vmem,
        compiler_params=pltpu.CompilerParams(vmem_limit_bytes=4 * 1024 * 1024),
        name="finish",
    )(came)


def narrow_kernel(hidden_ref, down_ref, out_ref, rows_ref):
    groups, rows, units = hidden_ref.shape
    blocks = down_ref.shape[0] // units
    total = jnp.zeros(out_ref.shape, f32)
    for b in range(blocks):
        for n in range(groups // blocks):
            place = (n % 2) * (groups // blocks // 2) + n // 2
            rows_ref[b, place * rows : (place + 1) * rows, :] = hidden_ref[n * blocks + b].astype(f32)
        total = total + jnp.dot(
            rows_ref[b].astype(bf16),
            down_ref[b * units : (b + 1) * units, :],
            preferred_element_type=f32,
        )
    out_ref[...] = total


def narrow(hidden, down_weight):
    groups, rows, units = hidden.shape
    blocks = down_weight.shape[0] // units
    all_rows = rows * groups // blocks
    vmem = pl.BlockSpec(memory_space=pltpu.VMEM)
    return pl.pallas_call(
        narrow_kernel,
        out_shape=jax.ShapeDtypeStruct((all_rows, down_weight.shape[1]), f32),
        in_specs=[vmem, vmem],
        out_specs=vmem,
        scratch_shapes=[pltpu.VMEM((blocks, all_rows, units), f32)],
        compiler_params=pltpu.CompilerParams(vmem_limit_bytes=8 * 1024 * 1024),
        name="narrow",
    )(hidden, down_weight)


def body(
    queries,
    new_key,
    new_value,
    key_pool,
    value_pool,
    page_table,
    lengths,
    residual,
    out_weight,
    norm_gain,
    gate_weight,
    up_weight,
    down_weight,
):
    shards = lax.axis_size(SHARD_AXES)
    groups = lax.axis_size(DP_AXES)
    near, far = lax.axis_size(NEAR_AXES), lax.axis_size(FAR_AXES)
    rows, width = residual.shape
    share_rows = rows // shards

    parts = attend(
        page_table,
        lengths,
        queries,
        new_key,
        new_value,
        key_pool.reshape(TOKENS, KVH * HD),
        value_pool.reshape(TOKENS, KVH * HD),
    )
    attended = merge(lax.all_to_all(parts, SHARD_AXES, 0, 0), groups)
    attended = lax.all_to_all(attended, DP_AXES, 0, 0)
    came = lax.all_to_all(project(attended, out_weight, shards), SHARD_AXES, 0, 0)
    sent, middle_own = widen(
        came, residual, norm_gain.reshape(1, width), gate_weight, up_weight, SPREAD_Y, share_rows
    )
    half = rows * SPREAD_Y // near
    came = lax.all_to_all(sent.reshape(near, half, sent.shape[2]), NEAR_AXES, 0, 0)
    sent = jnp.sum(came.astype(f32), axis=0).astype(bf16)
    came = lax.all_to_all(sent.reshape(far, half // far, sent.shape[1]), FAR_AXES, 0, 0)
    hidden = lax.all_to_all(finish(came, groups), DP_AXES, 0, 0)
    down = narrow(hidden, down_weight)
    down = lax.all_to_all(down.reshape(shards, share_rows, width), SHARD_AXES, 0, 0)
    return (middle_own + jnp.sum(down, axis=0)).astype(bf16)


def solution(mesh):
    lines, cores = mesh.shape["ctx"], mesh.shape["side"]
    split = Mesh(
        mesh.devices.reshape((2,) * len(DP_AXES) + (lines, cores)), DP_AXES + SHARD_AXES
    )
    dp, block = DP_AXES, SHARD_AXES
    placed = (
        P(dp, None),
        P(dp, None),
        P(dp, None),
        P(dp + block, None, None),
        P(dp + block, None, None),
        P(dp, block, None),
        P(dp),
        P(None, dp),
        P(block, dp),
        P(dp),
        P(dp, block),
        P(dp, block),
        P(block, dp),
    )
    return jax.shard_map(
        body, mesh=split, in_specs=placed, out_specs=P(block, dp), check_vma=False
    )
```

```python
import math

import jax
import jax.numpy as jnp
from jax import lax
from jax.experimental import pallas as pl
from jax.experimental.pallas import tpu as pltpu
from jax.sharding import Mesh
from jax.sharding import PartitionSpec as P

D = 8192
KVH = 8
HD = 128
PAGE = 64
PMAX = 12
G = 8
ROWS_DEV = 2
SLOTS = ROWS_DEV * PMAX
TOKENS = SLOTS * PAGE
PAIRS = KVH // 2
KEY_CHUNKS = 3
VALUE_CHUNKS = 3
PAIR_ROWS = 2 * ROWS_DEV * G
NEG = -1e30
SHARD_AXES = ("ctx", "side")
DP_AXES = ("z2", "z1", "z0", "y1", "y0")
NEAR_AXES = ("y1", "y0", "z0")
FAR_AXES = ("z2", "z1")
GATHER_AXES = ("z2", "z1", "z0", "y1", "y0")
UNIT_AXES = ("y1", "y0")
HALF_AXES = ("z0",)
ATTEND_VMEM = 64 * 1024 * 1024

norm_eps = 1e-05
f32 = jnp.float32
bf16 = jnp.bfloat16


def bits_of(index, axes):
    return {a: index >> (len(axes) - 1 - i) & 1 for i, a in enumerate(axes)}


def index_of(bits, axes):
    index = 0
    for a in axes:
        index = index * 2 + bits[a]
    return index


def attend_kernel(
    table_hbm, lengths_hbm, q_hbm, nk_hbm, nv_hbm, key_hbm, value_hbm, out_ref,
    table, lengths, q_two, nk_ref, nv_ref, q_rows, keys, values, scores, weights, owner,
    small_sem, key_sem, value_sem,
):
    shard = lax.axis_index(SHARD_AXES)
    small = [
        pltpu.make_async_copy(src, dst, small_sem.at[i])
        for i, (src, dst) in enumerate(
            [(q_hbm, q_two), (nk_hbm, nk_ref), (nv_hbm, nv_ref), (table_hbm, table), (lengths_hbm, lengths)]
        )
    ]
    for one in small:
        one.start()
    key_step, value_step = TOKENS // KEY_CHUNKS, TOKENS // VALUE_CHUNKS
    key_copies = [
        pltpu.make_async_copy(
            key_hbm.at[pl.ds(c * key_step, key_step)],
            keys.at[pl.ds(c * key_step, key_step)],
            key_sem.at[c],
        )
        for c in range(KEY_CHUNKS)
    ]
    value_copies = [
        pltpu.make_async_copy(
            value_hbm.at[pl.ds(c * value_step, value_step)],
            values.at[pl.ds(c * value_step, value_step)],
            value_sem.at[c],
        )
        for c in range(VALUE_CHUNKS)
    ]
    for copy in key_copies:
        copy.start()
    for one in small:
        one.wait()
    for copy in value_copies:
        copy.start()

    for k in range(SLOTS):
        owner[table[0, 0, k]] = k

    def limits_of(slot):
        k = owner[slot]
        own = lax.div(k, PMAX)
        start = (lax.rem(k, PMAX) * 8 + shard) * PAGE
        return [jnp.where(own == r, lengths[r] - start, 0) for r in range(ROWS_DEV)]

    q_all = q_two[...].astype(f32)
    for h in range(KVH):
        for r in range(ROWS_DEV):
            for g in range(G):
                at = (h // 2) * PAIR_ROWS + r * 2 * G + (h % 2) * G + g
                n = h * G + g
                q_rows[at : at + 1, :] = q_all[r : r + 1, n * HD : (n + 1) * HD]
    row = lax.broadcasted_iota(jnp.int32, (PAIR_ROWS, HD), 0)
    second = lax.rem(lax.div(row, G), 2) == 1

    lane = lax.broadcasted_iota(jnp.int32, (2 * G, HD), 1)
    within = lax.rem(lane, PAGE)
    first_half = lane < PAGE
    bias = []
    for t in range(TOKENS // HD):
        left, right = limits_of(2 * t), limits_of(2 * t + 1)
        halves = [
            jnp.where(within < jnp.where(first_half, left[r], right[r]), 0.0, NEG)
            for r in range(ROWS_DEV)
        ]
        bias.append(jnp.concatenate(halves, axis=0))
    bias = jnp.concatenate(bias, axis=1)

    def per_group(ref, j):
        parts = []
        for r in range(ROWS_DEV):
            for h in (2 * j, 2 * j + 1):
                one = ref[r : r + 1, h * HD : (h + 1) * HD].astype(f32)
                parts.append(jnp.broadcast_to(one, (G, HD)))
        return jnp.concatenate(parts, axis=0)

    scale = 1.0 / math.sqrt(HD)
    wides = []
    for j in range(PAIRS):
        q = q_rows[j * PAIR_ROWS : (j + 1) * PAIR_ROWS, :]
        wides.append(
            jnp.concatenate([jnp.where(second, 0.0, q), jnp.where(second, q, 0.0)], axis=1).astype(
                bf16
            )
        )
    for c in range(KEY_CHUNKS):
        key_copies[c].wait()
        tokens = slice(c * key_step, (c + 1) * key_step)
        for j in range(PAIRS):
            scores[j * PAIR_ROWS : (j + 1) * PAIR_ROWS, tokens] = bias[:, tokens] + lax.dot_general(
                wides[j],
                keys[tokens, j * 2 * HD : (j + 1) * 2 * HD],
                (((1,), (1,)), ((), ())),
                preferred_element_type=f32,
            )
    stat_lane = lax.broadcasted_iota(jnp.int32, (PAIR_ROWS, HD), 1)
    added, stats = [], []
    for j in range(PAIRS):
        rows = slice(j * PAIR_ROWS, (j + 1) * PAIR_ROWS)
        fresh = jnp.sum(q_rows[rows, :] * per_group(nk_ref, j), axis=1, keepdims=True)
        fresh = jnp.where(shard == 0, fresh, NEG)
        peak = jnp.maximum(jnp.max(scores[rows, :], axis=1, keepdims=True), fresh)
        peak = jnp.maximum(peak, 0.1 * NEG)
        weight = jnp.exp((scores[rows, :] - peak) * scale)
        fresh_weight = jnp.exp((fresh - peak) * scale)
        total = jnp.sum(weight, axis=1, keepdims=True) + fresh_weight
        weights[rows, :] = weight.astype(bf16)
        stats.append(jnp.where(stat_lane == 0, peak * scale, total))
        added.append(fresh_weight * per_group(nv_ref, j))
    mixed = [jnp.zeros((PAIR_ROWS, 2 * HD), f32) for _ in range(PAIRS)]
    for c in range(VALUE_CHUNKS):
        value_copies[c].wait()
        tokens = slice(c * value_step, (c + 1) * value_step)
        for j in range(PAIRS):
            mixed[j] = mixed[j] + jnp.dot(
                weights[j * PAIR_ROWS : (j + 1) * PAIR_ROWS, tokens],
                values[tokens, j * 2 * HD : (j + 1) * 2 * HD],
                preferred_element_type=f32,
            )
    for j in range(PAIRS):
        for r in range(ROWS_DEV):
            for n in range(2):
                at = (2 * r + n) * G
                rows = slice(r * G, (r + 1) * G)
                own = mixed[j][at : at + G, n * HD : (n + 1) * HD] + added[j][at : at + G, :]
                out_ref[2 * j + n, rows, 0:HD] = own
                out_ref[2 * j + n, rows, HD : 2 * HD] = stats[j][at : at + G, :]


def attend(table, lengths, q, new_key, new_value, keys, values):
    vmem = pl.BlockSpec(memory_space=pltpu.VMEM)
    hbm = pl.BlockSpec(memory_space=pltpu.HBM)
    return pl.pallas_call(
        attend_kernel,
        out_shape=jax.ShapeDtypeStruct((KVH, ROWS_DEV * G, 2 * HD), f32),
        in_specs=[hbm] * 7,
        out_specs=vmem,
        scratch_shapes=[
            pltpu.SMEM((1, 1, SLOTS), jnp.int32),
            pltpu.SMEM((ROWS_DEV,), jnp.int32),
            pltpu.VMEM((ROWS_DEV, KVH * G * HD), bf16),
            pltpu.VMEM((ROWS_DEV, KVH * HD), bf16),
            pltpu.VMEM((ROWS_DEV, KVH * HD), bf16),
            pltpu.VMEM((PAIRS * PAIR_ROWS, HD), f32),
            pltpu.VMEM((TOKENS, KVH * HD), bf16),
            pltpu.VMEM((TOKENS, KVH * HD), bf16),
            pltpu.VMEM((PAIRS * PAIR_ROWS, TOKENS), f32),
            pltpu.VMEM((PAIRS * PAIR_ROWS, TOKENS), bf16),
            pltpu.SMEM((SLOTS,), jnp.int32),
            pltpu.SemaphoreType.DMA((5,)),
            pltpu.SemaphoreType.DMA((KEY_CHUNKS,)),
            pltpu.SemaphoreType.DMA((VALUE_CHUNKS,)),
        ],
        compiler_params=pltpu.CompilerParams(vmem_limit_bytes=ATTEND_VMEM),
        name="attend",
    )(table, lengths, q, new_key, new_value, keys, values)


def merge_kernel(parts_ref, out_ref):
    shards = parts_ref.shape[0]
    peak = parts_ref[0, :, HD : HD + 1]
    for s in range(1, shards):
        peak = jnp.maximum(peak, parts_ref[s, :, HD : HD + 1])
    total = jnp.zeros_like(peak)
    mixed = jnp.zeros((ROWS_DEV * G, HD), f32)
    for s in range(shards):
        factor = jnp.exp(parts_ref[s, :, HD : HD + 1] - peak)
        total = total + factor * parts_ref[s, :, HD + 1 : HD + 2]
        mixed = mixed + factor * parts_ref[s, :, 0:HD]
    attended = (mixed / total).astype(bf16)
    for i in range(out_ref.shape[0]):
        out_ref[i] = attended


def merge(parts, copies):
    vmem = pl.BlockSpec(memory_space=pltpu.VMEM)
    return pl.pallas_call(
        merge_kernel,
        out_shape=jax.ShapeDtypeStruct((copies, ROWS_DEV * G, HD), bf16),
        in_specs=[vmem],
        out_specs=vmem,
        compiler_params=pltpu.CompilerParams(vmem_limit_bytes=4 * 1024 * 1024),
        cost_estimate=pl.CostEstimate(flops=20_000_000_000, bytes_accessed=0, transcendentals=0),
        name="merge",
    )(parts)


def project_kernel(attended_ref, weight_ref, out_ref, rows_ref):
    groups = attended_ref.shape[0]
    for n in range(groups):
        rows_ref[n * ROWS_DEV * G : (n + 1) * ROWS_DEV * G, :] = attended_ref[n].astype(f32)
    heads = [rows_ref[pl.ds(g, groups * ROWS_DEV, stride=G), :] for g in range(G)]
    wide = jnp.concatenate(heads, axis=1).astype(bf16)
    result = jnp.dot(wide, weight_ref[...], preferred_element_type=f32).astype(bf16)
    for i in range(out_ref.shape[0]):
        out_ref[i] = result


def project(attended, weight, copies):
    groups = attended.shape[0]
    vmem = pl.BlockSpec(memory_space=pltpu.VMEM)
    return pl.pallas_call(
        project_kernel,
        out_shape=jax.ShapeDtypeStruct((copies, groups * ROWS_DEV, weight.shape[1]), bf16),
        in_specs=[vmem, vmem],
        out_specs=vmem,
        scratch_shapes=[pltpu.VMEM((groups * ROWS_DEV * G, HD), f32)],
        compiler_params=pltpu.CompilerParams(vmem_limit_bytes=8 * 1024 * 1024),
        cost_estimate=pl.CostEstimate(flops=20_000_000_000, bytes_accessed=0, transcendentals=0),
        name="project",
    )(attended, weight)


def widen_kernel(
    came_ref, residual_ref, gain_ref, gate_ref, up_ref, sent_ref, own_ref, middle_ref
):
    projected = came_ref[0].astype(f32)
    for s in range(1, came_ref.shape[0]):
        projected = projected + came_ref[s].astype(f32)
    middle = (residual_ref[...].astype(f32) + projected).astype(bf16).astype(f32)
    middle_ref[...] = middle
    share = own_ref.shape[0]
    at = pl.multiple_of(lax.axis_index(SHARD_AXES) * share, share)
    own_ref[...] = middle_ref[pl.ds(at, share), :]
    scaled = (middle * gain_ref[...]).astype(bf16)
    squares = jnp.sum(middle * middle, axis=1, keepdims=True)
    high = squares.astype(bf16).astype(f32)
    lane = lax.broadcasted_iota(jnp.int32, (middle.shape[0], HD), 1)
    tail = jnp.where(lane == 0, high, jnp.where(lane == 1, squares - high, 0.0)).astype(bf16)
    blocks = 2 ** len(UNIT_AXES)
    half = sent_ref.shape[1]
    units = gate_ref.shape[1] // blocks
    targets = [bits_of(i, NEAR_AXES) for i in range(sent_ref.shape[0])]
    for b in range(blocks):
        parts = [
            jnp.dot(
                scaled, weight_ref[:, b * units : (b + 1) * units], preferred_element_type=f32
            ).astype(bf16)
            for weight_ref in (gate_ref, up_ref)
        ]
        for i, bits in enumerate(targets):
            if index_of(bits, UNIT_AXES) != b:
                continue
            at = index_of(bits, HALF_AXES) * half
            for n in range(2):
                sent_ref[i, :, n * units : (n + 1) * units] = parts[n][at : at + half, :]
            sent_ref[i, :, 2 * units :] = tail[at : at + half, :]


def widen(came, residual, gain, gate_weight, up_weight, share):
    rows, width = residual.shape
    members, halves = 2 ** len(NEAR_AXES), 2 ** len(HALF_AXES)
    units = gate_weight.shape[1] * halves // members
    vmem = pl.BlockSpec(memory_space=pltpu.VMEM)
    return pl.pallas_call(
        widen_kernel,
        out_shape=(
            jax.ShapeDtypeStruct((members, rows // halves, 2 * units + HD), bf16),
            jax.ShapeDtypeStruct((share, width), f32),
        ),
        in_specs=[vmem] * 5,
        out_specs=(vmem, vmem),
        scratch_shapes=[pltpu.VMEM((rows, width), f32)],
        compiler_params=pltpu.CompilerParams(vmem_limit_bytes=8 * 1024 * 1024),
        name="widen",
    )(came, residual, gain, gate_weight, up_weight)


def finish_kernel(came_ref, out_ref):
    units = out_ref.shape[2]
    sums = came_ref[0].astype(f32)
    for n in range(1, came_ref.shape[0]):
        sums = sums + came_ref[n].astype(f32)
    squares = sums[:, 2 * units : 2 * units + 1] + sums[:, 2 * units + 1 : 2 * units + 2]
    inverse = 1.0 / jnp.sqrt(squares / D + norm_eps)
    gate = sums[:, :units] * inverse
    up = sums[:, units : 2 * units] * inverse
    hidden = (gate / (1.0 + jnp.exp(-gate)) * up).astype(bf16)
    for n in range(out_ref.shape[0]):
        out_ref[n] = hidden


def finish(came, copies):
    _, rows, wide = came.shape
    vmem = pl.BlockSpec(memory_space=pltpu.VMEM)
    return pl.pallas_call(
        finish_kernel,
        out_shape=jax.ShapeDtypeStruct((copies, rows, (wide - HD) // 2), bf16),
        in_specs=[vmem],
        out_specs=vmem,
        compiler_params=pltpu.CompilerParams(vmem_limit_bytes=4 * 1024 * 1024),
        name="finish",
    )(came)


def narrow_kernel(hidden_ref, down_ref, out_ref, rows_ref):
    groups, rows, units = hidden_ref.shape
    blocks = down_ref.shape[0] // units
    total = jnp.zeros(out_ref.shape, f32)
    for b in range(blocks):
        for i in range(groups):
            bits = bits_of(i, GATHER_AXES)
            if index_of(bits, UNIT_AXES) == b:
                at = index_of(bits, HALF_AXES + FAR_AXES) * rows
                rows_ref[b, at : at + rows, :] = hidden_ref[i].astype(f32)
        total = total + jnp.dot(
            rows_ref[b].astype(bf16),
            down_ref[b * units : (b + 1) * units, :],
            preferred_element_type=f32,
        )
    out_ref[...] = total


def narrow(hidden, down_weight):
    groups, rows, units = hidden.shape
    blocks = down_weight.shape[0] // units
    all_rows = rows * groups // blocks
    vmem = pl.BlockSpec(memory_space=pltpu.VMEM)
    return pl.pallas_call(
        narrow_kernel,
        out_shape=jax.ShapeDtypeStruct((all_rows, down_weight.shape[1]), f32),
        in_specs=[vmem, vmem],
        out_specs=vmem,
        scratch_shapes=[pltpu.VMEM((blocks, all_rows, units), f32)],
        compiler_params=pltpu.CompilerParams(vmem_limit_bytes=8 * 1024 * 1024),
        name="narrow",
    )(hidden, down_weight)


def body(
    queries,
    new_key,
    new_value,
    key_pool,
    value_pool,
    page_table,
    lengths,
    residual,
    out_weight,
    norm_gain,
    gate_weight,
    up_weight,
    down_weight,
):
    shards = lax.axis_size(SHARD_AXES)
    groups = lax.axis_size(DP_AXES)
    far = lax.axis_size(FAR_AXES)
    rows, width = residual.shape
    share_rows = rows // shards

    parts = attend(
        page_table,
        lengths,
        queries,
        new_key,
        new_value,
        key_pool.reshape(TOKENS, KVH * HD),
        value_pool.reshape(TOKENS, KVH * HD),
    )
    attended = merge(lax.all_to_all(parts, SHARD_AXES, 0, 0), groups)
    attended = lax.all_to_all(attended, DP_AXES, 0, 0)
    came = lax.all_to_all(project(attended, out_weight, shards), SHARD_AXES, 0, 0)
    sent, middle_own = widen(
        came, residual, norm_gain.reshape(1, width), gate_weight, up_weight, share_rows
    )
    came = lax.all_to_all(sent, NEAR_AXES, 0, 0)
    sent = jnp.sum(came.astype(f32), axis=0).astype(bf16)
    came = lax.all_to_all(sent.reshape(far, sent.shape[0] // far, sent.shape[1]), FAR_AXES, 0, 0)
    hidden = lax.all_to_all(finish(came, groups), GATHER_AXES, 0, 0)
    down = narrow(hidden, down_weight)
    down = lax.all_to_all(down.reshape(shards, share_rows, width), SHARD_AXES, 0, 0)
    return (middle_own + jnp.sum(down, axis=0)).astype(bf16)


def solution(mesh):
    lines, cores = mesh.shape["ctx"], mesh.shape["side"]
    split = Mesh(
        mesh.devices.reshape((2,) * len(DP_AXES) + (lines, cores)), DP_AXES + SHARD_AXES
    )
    dp, block = DP_AXES, SHARD_AXES
    placed = (
        P(dp, None),
        P(dp, None),
        P(dp, None),
        P(dp + block, None, None),
        P(dp + block, None, None),
        P(dp, block, None),
        P(dp),
        P(None, dp),
        P(block, dp),
        P(dp),
        P(dp, block),
        P(dp, block),
        P(block, dp),
    )
    return jax.shard_map(
        body, mesh=split, in_specs=placed, out_specs=P(block, dp), check_vma=False
    )
```

```python
import math

import jax
import jax.numpy as jnp
from jax import lax
from jax.experimental import pallas as pl
from jax.experimental.pallas import tpu as pltpu
from jax.sharding import Mesh
from jax.sharding import PartitionSpec as P

D = 8192
KVH = 8
HD = 128
PAGE = 64
PMAX = 12
G = 8
ROWS_DEV = 2
SLOTS = ROWS_DEV * PMAX
TOKENS = SLOTS * PAGE
PAIRS = KVH // 2
KEY_CHUNKS = 3
VALUE_CHUNKS = 3
PAIR_ROWS = 2 * ROWS_DEV * G
NEG = -1e30
SHARD_AXES = ("ctx", "side")
DP_AXES = ("z2", "z1", "z0", "y1", "y0")
NEAR_AXES = ("y1", "y0", "z0")
FAR_AXES = ("z2", "z1")
GATHER_AXES = ("z2", "z1", "z0", "y1", "y0")
UNIT_AXES = ("y1", "y0")
HALF_AXES = ("z0",)
ATTEND_VMEM = 64 * 1024 * 1024

norm_eps = 1e-05
f32 = jnp.float32
bf16 = jnp.bfloat16


def bits_of(index, axes):
    return {a: index >> (len(axes) - 1 - i) & 1 for i, a in enumerate(axes)}


def index_of(bits, axes):
    index = 0
    for a in axes:
        index = index * 2 + bits[a]
    return index


def attend_kernel(
    table_hbm, lengths_hbm, q_hbm, nk_hbm, nv_hbm, key_hbm, value_hbm, out_ref,
    table, lengths, q_two, nk_ref, nv_ref, q_rows, keys, values, scores, weights, owner,
    small_sem, key_sem, value_sem,
):
    shard = lax.axis_index(SHARD_AXES)
    small = [
        pltpu.make_async_copy(src, dst, small_sem.at[i])
        for i, (src, dst) in enumerate(
            [(q_hbm, q_two), (nk_hbm, nk_ref), (nv_hbm, nv_ref), (table_hbm, table), (lengths_hbm, lengths)]
        )
    ]
    for one in small:
        one.start()
    key_step, value_step = TOKENS // KEY_CHUNKS, TOKENS // VALUE_CHUNKS
    key_copies = [
        pltpu.make_async_copy(
            key_hbm.at[pl.ds(c * key_step, key_step)],
            keys.at[pl.ds(c * key_step, key_step)],
            key_sem.at[c],
        )
        for c in range(KEY_CHUNKS)
    ]
    value_copies = [
        pltpu.make_async_copy(
            value_hbm.at[pl.ds(c * value_step, value_step)],
            values.at[pl.ds(c * value_step, value_step)],
            value_sem.at[c],
        )
        for c in range(VALUE_CHUNKS)
    ]
    for copy in key_copies:
        copy.start()
    for one in small:
        one.wait()
    for copy in value_copies:
        copy.start()

    for k in range(SLOTS):
        owner[table[0, 0, k]] = k

    def limits_of(slot):
        k = owner[slot]
        own = lax.div(k, PMAX)
        start = (lax.rem(k, PMAX) * 8 + shard) * PAGE
        return [jnp.where(own == r, lengths[r] - start, 0) for r in range(ROWS_DEV)]

    q_all = q_two[...].astype(f32)
    for h in range(KVH):
        for r in range(ROWS_DEV):
            for g in range(G):
                at = (h // 2) * PAIR_ROWS + r * 2 * G + (h % 2) * G + g
                n = h * G + g
                q_rows[at : at + 1, :] = q_all[r : r + 1, n * HD : (n + 1) * HD]
    row = lax.broadcasted_iota(jnp.int32, (PAIR_ROWS, HD), 0)
    second = lax.rem(lax.div(row, G), 2) == 1

    lane = lax.broadcasted_iota(jnp.int32, (2 * G, HD), 1)
    within = lax.rem(lane, PAGE)
    first_half = lane < PAGE
    bias = []
    for t in range(TOKENS // HD):
        left, right = limits_of(2 * t), limits_of(2 * t + 1)
        halves = [
            jnp.where(within < jnp.where(first_half, left[r], right[r]), 0.0, NEG)
            for r in range(ROWS_DEV)
        ]
        bias.append(jnp.concatenate(halves, axis=0))
    bias = jnp.concatenate(bias, axis=1)

    def per_group(ref, j):
        parts = []
        for r in range(ROWS_DEV):
            for h in (2 * j, 2 * j + 1):
                one = ref[r : r + 1, h * HD : (h + 1) * HD].astype(f32)
                parts.append(jnp.broadcast_to(one, (G, HD)))
        return jnp.concatenate(parts, axis=0)

    scale = 1.0 / math.sqrt(HD)
    wides = []
    for j in range(PAIRS):
        q = q_rows[j * PAIR_ROWS : (j + 1) * PAIR_ROWS, :]
        wides.append(
            jnp.concatenate([jnp.where(second, 0.0, q), jnp.where(second, q, 0.0)], axis=1).astype(
                bf16
            )
        )
    for c in range(KEY_CHUNKS):
        key_copies[c].wait()
        tokens = slice(c * key_step, (c + 1) * key_step)
        for j in range(PAIRS):
            scores[j * PAIR_ROWS : (j + 1) * PAIR_ROWS, tokens] = bias[:, tokens] + lax.dot_general(
                wides[j],
                keys[tokens, j * 2 * HD : (j + 1) * 2 * HD],
                (((1,), (1,)), ((), ())),
                preferred_element_type=f32,
            )
    stat_lane = lax.broadcasted_iota(jnp.int32, (PAIR_ROWS, HD), 1)
    added, stats = [], []
    for j in range(PAIRS):
        rows = slice(j * PAIR_ROWS, (j + 1) * PAIR_ROWS)
        fresh = jnp.sum(q_rows[rows, :] * per_group(nk_ref, j), axis=1, keepdims=True)
        fresh = jnp.where(shard == 0, fresh, NEG)
        peak = jnp.maximum(jnp.max(scores[rows, :], axis=1, keepdims=True), fresh)
        peak = jnp.maximum(peak, 0.1 * NEG)
        weight = jnp.exp((scores[rows, :] - peak) * scale)
        fresh_weight = jnp.exp((fresh - peak) * scale)
        total = jnp.sum(weight, axis=1, keepdims=True) + fresh_weight
        weights[rows, :] = weight.astype(bf16)
        own_stats = jnp.zeros((PAIR_ROWS, HD), f32)
        for n, value in enumerate((peak * scale, total)):
            rest = value
            for i in range(3):
                part = rest.astype(bf16).astype(f32)
                own_stats = jnp.where(stat_lane == 3 * n + i, part, own_stats)
                rest = rest - part
        stats.append(own_stats)
        added.append(fresh_weight * per_group(nv_ref, j))
    mixed = [jnp.zeros((PAIR_ROWS, 2 * HD), f32) for _ in range(PAIRS)]
    for c in range(VALUE_CHUNKS):
        value_copies[c].wait()
        tokens = slice(c * value_step, (c + 1) * value_step)
        for j in range(PAIRS):
            mixed[j] = mixed[j] + jnp.dot(
                weights[j * PAIR_ROWS : (j + 1) * PAIR_ROWS, tokens],
                values[tokens, j * 2 * HD : (j + 1) * 2 * HD],
                preferred_element_type=f32,
            )
    for j in range(PAIRS):
        for n in range(2):
            own, own_stats = [], []
            for r in range(ROWS_DEV):
                at = (2 * r + n) * G
                own.append(mixed[j][at : at + G, n * HD : (n + 1) * HD] + added[j][at : at + G, :])
                own_stats.append(stats[j][at : at + G, :])
            out_ref[2 * j + n, :, 0:HD] = jnp.concatenate(own, axis=0).astype(bf16)
            out_ref[2 * j + n, :, HD : 2 * HD] = jnp.concatenate(own_stats, axis=0).astype(bf16)


def attend(table, lengths, q, new_key, new_value, keys, values):
    vmem = pl.BlockSpec(memory_space=pltpu.VMEM)
    hbm = pl.BlockSpec(memory_space=pltpu.HBM)
    return pl.pallas_call(
        attend_kernel,
        out_shape=jax.ShapeDtypeStruct((KVH, ROWS_DEV * G, 2 * HD), bf16),
        in_specs=[hbm] * 7,
        out_specs=vmem,
        scratch_shapes=[
            pltpu.SMEM((1, 1, SLOTS), jnp.int32),
            pltpu.SMEM((ROWS_DEV,), jnp.int32),
            pltpu.VMEM((ROWS_DEV, KVH * G * HD), bf16),
            pltpu.VMEM((ROWS_DEV, KVH * HD), bf16),
            pltpu.VMEM((ROWS_DEV, KVH * HD), bf16),
            pltpu.VMEM((PAIRS * PAIR_ROWS, HD), f32),
            pltpu.VMEM((TOKENS, KVH * HD), bf16),
            pltpu.VMEM((TOKENS, KVH * HD), bf16),
            pltpu.VMEM((PAIRS * PAIR_ROWS, TOKENS), f32),
            pltpu.VMEM((PAIRS * PAIR_ROWS, TOKENS), bf16),
            pltpu.SMEM((SLOTS,), jnp.int32),
            pltpu.SemaphoreType.DMA((5,)),
            pltpu.SemaphoreType.DMA((KEY_CHUNKS,)),
            pltpu.SemaphoreType.DMA((VALUE_CHUNKS,)),
        ],
        compiler_params=pltpu.CompilerParams(vmem_limit_bytes=ATTEND_VMEM),
        name="attend",
    )(table, lengths, q, new_key, new_value, keys, values)


def merge_kernel(parts_ref, out_ref):
    shards = parts_ref.shape[0]
    peaks, totals = [], []
    for s in range(shards):
        stats = parts_ref[s, :, HD : 2 * HD].astype(f32)
        peaks.append(stats[:, 0:1] + stats[:, 1:2] + stats[:, 2:3])
        totals.append(stats[:, 3:4] + stats[:, 4:5] + stats[:, 5:6])
    peak = peaks[0]
    for s in range(1, shards):
        peak = jnp.maximum(peak, peaks[s])
    total = jnp.zeros_like(peak)
    mixed = jnp.zeros((ROWS_DEV * G, HD), f32)
    for s in range(shards):
        factor = jnp.exp(peaks[s] - peak)
        total = total + factor * totals[s]
        mixed = mixed + factor * parts_ref[s, :, 0:HD].astype(f32)
    attended = (mixed / total).astype(bf16)
    for i in range(out_ref.shape[0]):
        out_ref[i] = attended


def merge(parts, copies):
    vmem = pl.BlockSpec(memory_space=pltpu.VMEM)
    return pl.pallas_call(
        merge_kernel,
        out_shape=jax.ShapeDtypeStruct((copies, ROWS_DEV * G, HD), bf16),
        in_specs=[vmem],
        out_specs=vmem,
        compiler_params=pltpu.CompilerParams(vmem_limit_bytes=4 * 1024 * 1024),
        cost_estimate=pl.CostEstimate(flops=20_000_000_000, bytes_accessed=0, transcendentals=0),
        name="merge",
    )(parts)


def project_kernel(attended_ref, weight_ref, out_ref, rows_ref):
    groups = attended_ref.shape[0]
    for n in range(groups):
        rows_ref[n * ROWS_DEV * G : (n + 1) * ROWS_DEV * G, :] = attended_ref[n].astype(f32)
    heads = [rows_ref[pl.ds(g, groups * ROWS_DEV, stride=G), :] for g in range(G)]
    wide = jnp.concatenate(heads, axis=1).astype(bf16)
    result = jnp.dot(wide, weight_ref[...], preferred_element_type=f32).astype(bf16)
    for i in range(out_ref.shape[0]):
        out_ref[i] = result


def project(attended, weight, copies):
    groups = attended.shape[0]
    vmem = pl.BlockSpec(memory_space=pltpu.VMEM)
    return pl.pallas_call(
        project_kernel,
        out_shape=jax.ShapeDtypeStruct((copies, groups * ROWS_DEV, weight.shape[1]), bf16),
        in_specs=[vmem, vmem],
        out_specs=vmem,
        scratch_shapes=[pltpu.VMEM((groups * ROWS_DEV * G, HD), f32)],
        compiler_params=pltpu.CompilerParams(vmem_limit_bytes=8 * 1024 * 1024),
        cost_estimate=pl.CostEstimate(flops=20_000_000_000, bytes_accessed=0, transcendentals=0),
        name="project",
    )(attended, weight)


def widen_kernel(
    came_ref, residual_ref, gain_ref, gate_ref, up_ref, sent_ref, own_ref, middle_ref
):
    projected = came_ref[0].astype(f32)
    for s in range(1, came_ref.shape[0]):
        projected = projected + came_ref[s].astype(f32)
    middle = (residual_ref[...].astype(f32) + projected).astype(bf16).astype(f32)
    middle_ref[...] = middle
    share = own_ref.shape[0]
    at = pl.multiple_of(lax.axis_index(SHARD_AXES) * share, share)
    own_ref[...] = middle_ref[pl.ds(at, share), :]
    scaled = (middle * gain_ref[...]).astype(bf16)
    squares = jnp.sum(middle * middle, axis=1, keepdims=True)
    high = squares.astype(bf16).astype(f32)
    lane = lax.broadcasted_iota(jnp.int32, (middle.shape[0], HD), 1)
    tail = jnp.where(lane == 0, high, jnp.where(lane == 1, squares - high, 0.0)).astype(bf16)
    blocks = 2 ** len(UNIT_AXES)
    half = sent_ref.shape[1]
    units = gate_ref.shape[1] // blocks
    targets = [bits_of(i, NEAR_AXES) for i in range(sent_ref.shape[0])]
    for b in range(blocks):
        parts = [
            jnp.dot(
                scaled, weight_ref[:, b * units : (b + 1) * units], preferred_element_type=f32
            ).astype(bf16)
            for weight_ref in (gate_ref, up_ref)
        ]
        for i, bits in enumerate(targets):
            if index_of(bits, UNIT_AXES) != b:
                continue
            at = index_of(bits, HALF_AXES) * half
            for n in range(2):
                sent_ref[i, :, n * units : (n + 1) * units] = parts[n][at : at + half, :]
            sent_ref[i, :, 2 * units :] = tail[at : at + half, :]


def widen(came, residual, gain, gate_weight, up_weight, share):
    rows, width = residual.shape
    members, halves = 2 ** len(NEAR_AXES), 2 ** len(HALF_AXES)
    units = gate_weight.shape[1] * halves // members
    vmem = pl.BlockSpec(memory_space=pltpu.VMEM)
    return pl.pallas_call(
        widen_kernel,
        out_shape=(
            jax.ShapeDtypeStruct((members, rows // halves, 2 * units + HD), bf16),
            jax.ShapeDtypeStruct((share, width), f32),
        ),
        in_specs=[vmem] * 5,
        out_specs=(vmem, vmem),
        scratch_shapes=[pltpu.VMEM((rows, width), f32)],
        compiler_params=pltpu.CompilerParams(vmem_limit_bytes=8 * 1024 * 1024),
        name="widen",
    )(came, residual, gain, gate_weight, up_weight)


def finish_kernel(came_ref, out_ref):
    units = out_ref.shape[2]
    sums = came_ref[0].astype(f32)
    for n in range(1, came_ref.shape[0]):
        sums = sums + came_ref[n].astype(f32)
    squares = sums[:, 2 * units : 2 * units + 1] + sums[:, 2 * units + 1 : 2 * units + 2]
    inverse = 1.0 / jnp.sqrt(squares / D + norm_eps)
    gate = sums[:, :units] * inverse
    up = sums[:, units : 2 * units] * inverse
    hidden = (gate / (1.0 + jnp.exp(-gate)) * up).astype(bf16)
    for n in range(out_ref.shape[0]):
        out_ref[n] = hidden


def finish(came, copies):
    _, rows, wide = came.shape
    vmem = pl.BlockSpec(memory_space=pltpu.VMEM)
    return pl.pallas_call(
        finish_kernel,
        out_shape=jax.ShapeDtypeStruct((copies, rows, (wide - HD) // 2), bf16),
        in_specs=[vmem],
        out_specs=vmem,
        compiler_params=pltpu.CompilerParams(vmem_limit_bytes=4 * 1024 * 1024),
        name="finish",
    )(came)


def narrow_kernel(hidden_ref, down_ref, out_ref, rows_ref):
    groups, rows, units = hidden_ref.shape
    blocks = down_ref.shape[0] // units
    total = jnp.zeros(out_ref.shape, f32)
    for b in range(blocks):
        for i in range(groups):
            bits = bits_of(i, GATHER_AXES)
            if index_of(bits, UNIT_AXES) == b:
                at = index_of(bits, HALF_AXES + FAR_AXES) * rows
                rows_ref[b, at : at + rows, :] = hidden_ref[i].astype(f32)
        total = total + jnp.dot(
            rows_ref[b].astype(bf16),
            down_ref[b * units : (b + 1) * units, :],
            preferred_element_type=f32,
        )
    out_ref[...] = total.astype(bf16)


def narrow(hidden, down_weight):
    groups, rows, units = hidden.shape
    blocks = down_weight.shape[0] // units
    all_rows = rows * groups // blocks
    vmem = pl.BlockSpec(memory_space=pltpu.VMEM)
    return pl.pallas_call(
        narrow_kernel,
        out_shape=jax.ShapeDtypeStruct((all_rows, down_weight.shape[1]), bf16),
        in_specs=[vmem, vmem],
        out_specs=vmem,
        scratch_shapes=[pltpu.VMEM((blocks, all_rows, units), f32)],
        compiler_params=pltpu.CompilerParams(vmem_limit_bytes=8 * 1024 * 1024),
        name="narrow",
    )(hidden, down_weight)


def body(
    queries,
    new_key,
    new_value,
    key_pool,
    value_pool,
    page_table,
    lengths,
    residual,
    out_weight,
    norm_gain,
    gate_weight,
    up_weight,
    down_weight,
):
    shards = lax.axis_size(SHARD_AXES)
    groups = lax.axis_size(DP_AXES)
    far = lax.axis_size(FAR_AXES)
    rows, width = residual.shape
    share_rows = rows // shards

    parts = attend(
        page_table,
        lengths,
        queries,
        new_key,
        new_value,
        key_pool.reshape(TOKENS, KVH * HD),
        value_pool.reshape(TOKENS, KVH * HD),
    )
    attended = merge(lax.all_to_all(parts, SHARD_AXES, 0, 0), groups)
    attended = lax.all_to_all(attended, DP_AXES, 0, 0)
    came = lax.all_to_all(project(attended, out_weight, shards), SHARD_AXES, 0, 0)
    sent, middle_own = widen(
        came, residual, norm_gain.reshape(1, width), gate_weight, up_weight, share_rows
    )
    came = lax.all_to_all(sent, NEAR_AXES, 0, 0)
    sent = jnp.sum(came.astype(f32), axis=0).astype(bf16)
    came = lax.all_to_all(sent.reshape(far, sent.shape[0] // far, sent.shape[1]), FAR_AXES, 0, 0)
    hidden = lax.all_to_all(finish(came, groups), GATHER_AXES, 0, 0)
    down = narrow(hidden, down_weight)
    down = lax.all_to_all(down.reshape(shards, share_rows, width), SHARD_AXES, 0, 0)
    return (middle_own + jnp.sum(down.astype(f32), axis=0)).astype(bf16)


def solution(mesh):
    lines, cores = mesh.shape["ctx"], mesh.shape["side"]
    split = Mesh(
        mesh.devices.reshape((2,) * len(DP_AXES) + (lines, cores)), DP_AXES + SHARD_AXES
    )
    dp, block = DP_AXES, SHARD_AXES
    placed = (
        P(dp, None),
        P(dp, None),
        P(dp, None),
        P(dp + block, None, None),
        P(dp + block, None, None),
        P(dp, block, None),
        P(dp),
        P(None, dp),
        P(block, dp),
        P(dp),
        P(dp, block),
        P(dp, block),
        P(block, dp),
    )
    return jax.shard_map(
        body, mesh=split, in_specs=placed, out_specs=P(block, dp), check_vma=False
    )
```

```python
import itertools
import math

import jax
import jax.numpy as jnp
from jax import lax
from jax.experimental import pallas as pl
from jax.experimental.pallas import tpu as pltpu
from jax.sharding import Mesh
from jax.sharding import PartitionSpec as P

D = 8192
KVH = 8
HD = 128
PAGE = 64
PMAX = 12
G = 8
ROWS_DEV = 2
SLOTS = ROWS_DEV * PMAX
TOKENS = SLOTS * PAGE
PAIRS = KVH // 2
KEY_CHUNKS = 3
VALUE_CHUNKS = 3
PAIR_ROWS = 2 * ROWS_DEV * G
NEG = -1e30
SHARD_AXES = ("ctx", "side")
SHARD_SIZES = (4, 2)
DP_AXES = ("z2", "z1", "z0", "y1", "y0")
NEAR_AXES = ("y1", "y0", "z0")
FAR_AXES = ("z2", "z1")
GATHER_AXES = ("z2", "z1", "z0", "y1", "y0")
UNIT_AXES = ("y1", "y0")
Z_AXES = ("z2", "z1", "z0")
HALF_AXES = ("z0",)
ATTEND_VMEM = 64 * 1024 * 1024

norm_eps = 1e-05
f32 = jnp.float32
bf16 = jnp.bfloat16


def bits_of(index, axes):
    return {a: index >> (len(axes) - 1 - i) & 1 for i, a in enumerate(axes)}


def gather_members():
    members = []
    for i in range(2 ** len(GATHER_AXES)):
        z, y = i % 8, (i + i // 8) % 4
        members.append({**bits_of(z, Z_AXES), **bits_of(y, UNIT_AXES)})
    return members


def index_of(bits, axes):
    index = 0
    for a in axes:
        index = index * 2 + bits[a]
    return index


def in_order(members, axes):
    names = DP_AXES + SHARD_AXES
    sizes = (2,) * len(DP_AXES) + SHARD_SIZES
    rest = [i for i, a in enumerate(names) if a not in axes]
    order = []
    for fixed in itertools.product(*(range(sizes[i]) for i in rest)):
        group = []
        for bits in members:
            device = 0
            for i, a in enumerate(names):
                device = device * sizes[i] + (bits[a] if a in bits else fixed[rest.index(i)])
            group.append(device)
        order.append(group)
    return order


def swap(x, members, axes):
    return lax.all_to_all(
        x, DP_AXES + SHARD_AXES, 0, 0, axis_index_groups=in_order(members, axes)
    )


def attend_kernel(
    table_hbm, lengths_hbm, q_hbm, nk_hbm, nv_hbm, key_hbm, value_hbm, out_ref,
    table, lengths, q_two, nk_ref, nv_ref, q_rows, keys, values, scores, weights, owner,
    small_sem, key_sem, value_sem,
):
    shard = lax.axis_index(SHARD_AXES)
    small = [
        pltpu.make_async_copy(src, dst, small_sem.at[i])
        for i, (src, dst) in enumerate(
            [(q_hbm, q_two), (nk_hbm, nk_ref), (nv_hbm, nv_ref), (table_hbm, table), (lengths_hbm, lengths)]
        )
    ]
    for one in small:
        one.start()
    key_step, value_step = TOKENS // KEY_CHUNKS, TOKENS // VALUE_CHUNKS
    key_copies = [
        pltpu.make_async_copy(
            key_hbm.at[pl.ds(c * key_step, key_step)],
            keys.at[pl.ds(c * key_step, key_step)],
            key_sem.at[c],
        )
        for c in range(KEY_CHUNKS)
    ]
    value_copies = [
        pltpu.make_async_copy(
            value_hbm.at[pl.ds(c * value_step, value_step)],
            values.at[pl.ds(c * value_step, value_step)],
            value_sem.at[c],
        )
        for c in range(VALUE_CHUNKS)
    ]
    for copy in key_copies:
        copy.start()
    for one in small:
        one.wait()
    for copy in value_copies:
        copy.start()

    for k in range(SLOTS):
        owner[table[0, 0, k]] = k

    def limits_of(slot):
        k = owner[slot]
        own = lax.div(k, PMAX)
        start = (lax.rem(k, PMAX) * 8 + shard) * PAGE
        return [jnp.where(own == r, lengths[r] - start, 0) for r in range(ROWS_DEV)]

    q_all = q_two[...].astype(f32)
    for h in range(KVH):
        for r in range(ROWS_DEV):
            for g in range(G):
                at = (h // 2) * PAIR_ROWS + r * 2 * G + (h % 2) * G + g
                n = h * G + g
                q_rows[at : at + 1, :] = q_all[r : r + 1, n * HD : (n + 1) * HD]
    row = lax.broadcasted_iota(jnp.int32, (PAIR_ROWS, HD), 0)
    second = lax.rem(lax.div(row, G), 2) == 1

    lane = lax.broadcasted_iota(jnp.int32, (2 * G, HD), 1)
    within = lax.rem(lane, PAGE)
    first_half = lane < PAGE
    bias = []
    for t in range(TOKENS // HD):
        left, right = limits_of(2 * t), limits_of(2 * t + 1)
        halves = [
            jnp.where(within < jnp.where(first_half, left[r], right[r]), 0.0, NEG)
            for r in range(ROWS_DEV)
        ]
        bias.append(jnp.concatenate(halves, axis=0))
    bias = jnp.concatenate(bias, axis=1)

    def per_group(ref, j):
        parts = []
        for r in range(ROWS_DEV):
            for h in (2 * j, 2 * j + 1):
                one = ref[r : r + 1, h * HD : (h + 1) * HD].astype(f32)
                parts.append(jnp.broadcast_to(one, (G, HD)))
        return jnp.concatenate(parts, axis=0)

    scale = 1.0 / math.sqrt(HD)
    wides = []
    for j in range(PAIRS):
        q = q_rows[j * PAIR_ROWS : (j + 1) * PAIR_ROWS, :]
        wides.append(
            jnp.concatenate([jnp.where(second, 0.0, q), jnp.where(second, q, 0.0)], axis=1).astype(
                bf16
            )
        )
    for c in range(KEY_CHUNKS):
        key_copies[c].wait()
        tokens = slice(c * key_step, (c + 1) * key_step)
        for j in range(PAIRS):
            scores[j * PAIR_ROWS : (j + 1) * PAIR_ROWS, tokens] = bias[:, tokens] + lax.dot_general(
                wides[j],
                keys[tokens, j * 2 * HD : (j + 1) * 2 * HD],
                (((1,), (1,)), ((), ())),
                preferred_element_type=f32,
            )
    stat_lane = lax.broadcasted_iota(jnp.int32, (PAIR_ROWS, HD), 1)
    added, stats = [], []
    for j in range(PAIRS):
        rows = slice(j * PAIR_ROWS, (j + 1) * PAIR_ROWS)
        fresh = jnp.sum(q_rows[rows, :] * per_group(nk_ref, j), axis=1, keepdims=True)
        fresh = jnp.where(shard == 0, fresh, NEG)
        peak = jnp.maximum(jnp.max(scores[rows, :], axis=1, keepdims=True), fresh)
        peak = jnp.maximum(peak, 0.1 * NEG)
        weight = jnp.exp((scores[rows, :] - peak) * scale)
        fresh_weight = jnp.exp((fresh - peak) * scale)
        total = jnp.sum(weight, axis=1, keepdims=True) + fresh_weight
        weights[rows, :] = weight.astype(bf16)
        own_stats = jnp.zeros((PAIR_ROWS, HD), f32)
        for n, value in enumerate((peak * scale, total)):
            rest = value
            for i in range(3):
                part = rest.astype(bf16).astype(f32)
                own_stats = jnp.where(stat_lane == 3 * n + i, part, own_stats)
                rest = rest - part
        stats.append(own_stats)
        added.append(fresh_weight * per_group(nv_ref, j))
    mixed = [jnp.zeros((PAIR_ROWS, 2 * HD), f32) for _ in range(PAIRS)]
    for c in range(VALUE_CHUNKS):
        value_copies[c].wait()
        tokens = slice(c * value_step, (c + 1) * value_step)
        for j in range(PAIRS):
            mixed[j] = mixed[j] + jnp.dot(
                weights[j * PAIR_ROWS : (j + 1) * PAIR_ROWS, tokens],
                values[tokens, j * 2 * HD : (j + 1) * 2 * HD],
                preferred_element_type=f32,
            )
    for j in range(PAIRS):
        for n in range(2):
            own, own_stats = [], []
            for r in range(ROWS_DEV):
                at = (2 * r + n) * G
                own.append(mixed[j][at : at + G, n * HD : (n + 1) * HD] + added[j][at : at + G, :])
                own_stats.append(stats[j][at : at + G, :])
            out_ref[2 * j + n, :, 0:HD] = jnp.concatenate(own, axis=0).astype(bf16)
            out_ref[2 * j + n, :, HD : 2 * HD] = jnp.concatenate(own_stats, axis=0).astype(bf16)


def attend(table, lengths, q, new_key, new_value, keys, values):
    vmem = pl.BlockSpec(memory_space=pltpu.VMEM)
    hbm = pl.BlockSpec(memory_space=pltpu.HBM)
    return pl.pallas_call(
        attend_kernel,
        out_shape=jax.ShapeDtypeStruct((KVH, ROWS_DEV * G, 2 * HD), bf16),
        in_specs=[hbm] * 7,
        out_specs=vmem,
        scratch_shapes=[
            pltpu.SMEM((1, 1, SLOTS), jnp.int32),
            pltpu.SMEM((ROWS_DEV,), jnp.int32),
            pltpu.VMEM((ROWS_DEV, KVH * G * HD), bf16),
            pltpu.VMEM((ROWS_DEV, KVH * HD), bf16),
            pltpu.VMEM((ROWS_DEV, KVH * HD), bf16),
            pltpu.VMEM((PAIRS * PAIR_ROWS, HD), f32),
            pltpu.VMEM((TOKENS, KVH * HD), bf16),
            pltpu.VMEM((TOKENS, KVH * HD), bf16),
            pltpu.VMEM((PAIRS * PAIR_ROWS, TOKENS), f32),
            pltpu.VMEM((PAIRS * PAIR_ROWS, TOKENS), bf16),
            pltpu.SMEM((SLOTS,), jnp.int32),
            pltpu.SemaphoreType.DMA((5,)),
            pltpu.SemaphoreType.DMA((KEY_CHUNKS,)),
            pltpu.SemaphoreType.DMA((VALUE_CHUNKS,)),
        ],
        compiler_params=pltpu.CompilerParams(vmem_limit_bytes=ATTEND_VMEM),
        name="attend",
    )(table, lengths, q, new_key, new_value, keys, values)


def merge_kernel(parts_ref, out_ref):
    shards = parts_ref.shape[0]
    peaks, totals = [], []
    for s in range(shards):
        stats = parts_ref[s, :, HD : 2 * HD].astype(f32)
        peaks.append(stats[:, 0:1] + stats[:, 1:2] + stats[:, 2:3])
        totals.append(stats[:, 3:4] + stats[:, 4:5] + stats[:, 5:6])
    peak = peaks[0]
    for s in range(1, shards):
        peak = jnp.maximum(peak, peaks[s])
    total = jnp.zeros_like(peak)
    mixed = jnp.zeros((ROWS_DEV * G, HD), f32)
    for s in range(shards):
        factor = jnp.exp(peaks[s] - peak)
        total = total + factor * totals[s]
        mixed = mixed + factor * parts_ref[s, :, 0:HD].astype(f32)
    attended = (mixed / total).astype(bf16)
    for i in range(out_ref.shape[0]):
        out_ref[i] = attended


def merge(parts, copies):
    vmem = pl.BlockSpec(memory_space=pltpu.VMEM)
    return pl.pallas_call(
        merge_kernel,
        out_shape=jax.ShapeDtypeStruct((copies, ROWS_DEV * G, HD), bf16),
        in_specs=[vmem],
        out_specs=vmem,
        compiler_params=pltpu.CompilerParams(vmem_limit_bytes=4 * 1024 * 1024),
        cost_estimate=pl.CostEstimate(flops=20_000_000_000, bytes_accessed=0, transcendentals=0),
        name="merge",
    )(parts)


def project_kernel(attended_ref, weight_ref, out_ref, rows_ref):
    groups = attended_ref.shape[0]
    for n in range(groups):
        rows_ref[n * ROWS_DEV * G : (n + 1) * ROWS_DEV * G, :] = attended_ref[n].astype(f32)
    heads = [rows_ref[pl.ds(g, groups * ROWS_DEV, stride=G), :] for g in range(G)]
    wide = jnp.concatenate(heads, axis=1).astype(bf16)
    result = jnp.dot(wide, weight_ref[...], preferred_element_type=f32).astype(bf16)
    for i in range(out_ref.shape[0]):
        out_ref[i] = result


def project(attended, weight, copies):
    groups = attended.shape[0]
    vmem = pl.BlockSpec(memory_space=pltpu.VMEM)
    return pl.pallas_call(
        project_kernel,
        out_shape=jax.ShapeDtypeStruct((copies, groups * ROWS_DEV, weight.shape[1]), bf16),
        in_specs=[vmem, vmem],
        out_specs=vmem,
        scratch_shapes=[pltpu.VMEM((groups * ROWS_DEV * G, HD), f32)],
        compiler_params=pltpu.CompilerParams(vmem_limit_bytes=8 * 1024 * 1024),
        cost_estimate=pl.CostEstimate(flops=20_000_000_000, bytes_accessed=0, transcendentals=0),
        name="project",
    )(attended, weight)


def widen_kernel(
    came_ref, residual_ref, gain_ref, gate_ref, up_ref, sent_ref, own_ref, middle_ref
):
    projected = came_ref[0].astype(f32)
    for s in range(1, came_ref.shape[0]):
        projected = projected + came_ref[s].astype(f32)
    middle = (residual_ref[...].astype(f32) + projected).astype(bf16).astype(f32)
    middle_ref[...] = middle
    share = own_ref.shape[0]
    at = pl.multiple_of(lax.axis_index(SHARD_AXES) * share, share)
    own_ref[...] = middle_ref[pl.ds(at, share), :]
    scaled = (middle * gain_ref[...]).astype(bf16)
    squares = jnp.sum(middle * middle, axis=1, keepdims=True)
    high = squares.astype(bf16).astype(f32)
    lane = lax.broadcasted_iota(jnp.int32, (middle.shape[0], HD), 1)
    tail = jnp.where(lane == 0, high, jnp.where(lane == 1, squares - high, 0.0)).astype(bf16)
    blocks = 2 ** len(UNIT_AXES)
    half = sent_ref.shape[1]
    units = gate_ref.shape[1] // blocks
    targets = [bits_of(i, NEAR_AXES) for i in range(sent_ref.shape[0])]
    for b in range(blocks):
        parts = [
            jnp.dot(
                scaled, weight_ref[:, b * units : (b + 1) * units], preferred_element_type=f32
            ).astype(bf16)
            for weight_ref in (gate_ref, up_ref)
        ]
        for i, bits in enumerate(targets):
            if index_of(bits, UNIT_AXES) != b:
                continue
            at = index_of(bits, HALF_AXES) * half
            for n in range(2):
                sent_ref[i, :, n * units : (n + 1) * units] = parts[n][at : at + half, :]
            sent_ref[i, :, 2 * units :] = tail[at : at + half, :]


def widen(came, residual, gain, gate_weight, up_weight, share):
    rows, width = residual.shape
    members, halves = 2 ** len(NEAR_AXES), 2 ** len(HALF_AXES)
    units = gate_weight.shape[1] * halves // members
    vmem = pl.BlockSpec(memory_space=pltpu.VMEM)
    return pl.pallas_call(
        widen_kernel,
        out_shape=(
            jax.ShapeDtypeStruct((members, rows // halves, 2 * units + HD), bf16),
            jax.ShapeDtypeStruct((share, width), f32),
        ),
        in_specs=[vmem] * 5,
        out_specs=(vmem, vmem),
        scratch_shapes=[pltpu.VMEM((rows, width), f32)],
        compiler_params=pltpu.CompilerParams(vmem_limit_bytes=8 * 1024 * 1024),
        name="widen",
    )(came, residual, gain, gate_weight, up_weight)


def finish_kernel(came_ref, out_ref):
    units = out_ref.shape[2]
    sums = came_ref[0].astype(f32)
    for n in range(1, came_ref.shape[0]):
        sums = sums + came_ref[n].astype(f32)
    squares = sums[:, 2 * units : 2 * units + 1] + sums[:, 2 * units + 1 : 2 * units + 2]
    inverse = 1.0 / jnp.sqrt(squares / D + norm_eps)
    gate = sums[:, :units] * inverse
    up = sums[:, units : 2 * units] * inverse
    hidden = (gate / (1.0 + jnp.exp(-gate)) * up).astype(bf16)
    for n in range(out_ref.shape[0]):
        out_ref[n] = hidden


def finish(came, copies):
    _, rows, wide = came.shape
    vmem = pl.BlockSpec(memory_space=pltpu.VMEM)
    return pl.pallas_call(
        finish_kernel,
        out_shape=jax.ShapeDtypeStruct((copies, rows, (wide - HD) // 2), bf16),
        in_specs=[vmem],
        out_specs=vmem,
        compiler_params=pltpu.CompilerParams(vmem_limit_bytes=4 * 1024 * 1024),
        name="finish",
    )(came)


def narrow_kernel(hidden_ref, down_ref, out_ref, rows_ref):
    groups, rows, units = hidden_ref.shape
    blocks = down_ref.shape[0] // units
    total = jnp.zeros(out_ref.shape, f32)
    for b in range(blocks):
        for i in range(groups):
            bits = gather_members()[i]
            if index_of(bits, UNIT_AXES) == b:
                at = index_of(bits, HALF_AXES + FAR_AXES) * rows
                rows_ref[b, at : at + rows, :] = hidden_ref[i].astype(f32)
        total = total + jnp.dot(
            rows_ref[b].astype(bf16),
            down_ref[b * units : (b + 1) * units, :],
            preferred_element_type=f32,
        )
    out_ref[...] = total.astype(bf16)


def narrow(hidden, down_weight):
    groups, rows, units = hidden.shape
    blocks = down_weight.shape[0] // units
    all_rows = rows * groups // blocks
    vmem = pl.BlockSpec(memory_space=pltpu.VMEM)
    return pl.pallas_call(
        narrow_kernel,
        out_shape=jax.ShapeDtypeStruct((all_rows, down_weight.shape[1]), bf16),
        in_specs=[vmem, vmem],
        out_specs=vmem,
        scratch_shapes=[pltpu.VMEM((blocks, all_rows, units), f32)],
        compiler_params=pltpu.CompilerParams(vmem_limit_bytes=8 * 1024 * 1024),
        name="narrow",
    )(hidden, down_weight)


def body(
    queries,
    new_key,
    new_value,
    key_pool,
    value_pool,
    page_table,
    lengths,
    residual,
    out_weight,
    norm_gain,
    gate_weight,
    up_weight,
    down_weight,
):
    shards = lax.axis_size(SHARD_AXES)
    groups = lax.axis_size(DP_AXES)
    far = lax.axis_size(FAR_AXES)
    rows, width = residual.shape
    share_rows = rows // shards

    parts = attend(
        page_table,
        lengths,
        queries,
        new_key,
        new_value,
        key_pool.reshape(TOKENS, KVH * HD),
        value_pool.reshape(TOKENS, KVH * HD),
    )
    attended = merge(lax.all_to_all(parts, SHARD_AXES, 0, 0), groups)
    attended = lax.all_to_all(attended, DP_AXES, 0, 0)
    came = lax.all_to_all(project(attended, out_weight, shards), SHARD_AXES, 0, 0)
    sent, middle_own = widen(
        came, residual, norm_gain.reshape(1, width), gate_weight, up_weight, share_rows
    )
    came = lax.all_to_all(sent, NEAR_AXES, 0, 0)
    sent = jnp.sum(came.astype(f32), axis=0).astype(bf16)
    came = lax.all_to_all(sent.reshape(far, sent.shape[0] // far, sent.shape[1]), FAR_AXES, 0, 0)
    hidden = swap(finish(came, groups), gather_members(), GATHER_AXES)
    down = narrow(hidden, down_weight)
    down = lax.all_to_all(down.reshape(shards, share_rows, width), SHARD_AXES, 0, 0)
    return (middle_own + jnp.sum(down.astype(f32), axis=0)).astype(bf16)


def solution(mesh):
    lines, cores = mesh.shape["ctx"], mesh.shape["side"]
    split = Mesh(
        mesh.devices.reshape((2,) * len(DP_AXES) + (lines, cores)), DP_AXES + SHARD_AXES
    )
    dp, block = DP_AXES, SHARD_AXES
    placed = (
        P(dp, None),
        P(dp, None),
        P(dp, None),
        P(dp + block, None, None),
        P(dp + block, None, None),
        P(dp, block, None),
        P(dp),
        P(None, dp),
        P(block, dp),
        P(dp),
        P(dp, block),
        P(dp, block),
        P(block, dp),
    )
    return jax.shard_map(
        body, mesh=split, in_specs=placed, out_specs=P(block, dp), check_vma=False
    )
```

```python
import itertools
import math

import jax
import jax.numpy as jnp
from jax import lax
from jax.experimental import pallas as pl
from jax.experimental.pallas import tpu as pltpu
from jax.sharding import Mesh
from jax.sharding import PartitionSpec as P

D = 8192
KVH = 8
HD = 128
PAGE = 64
PMAX = 12
G = 8
ROWS_DEV = 2
SLOTS = ROWS_DEV * PMAX
TOKENS = SLOTS * PAGE
PAIRS = KVH // 2
KEY_CHUNKS = 3
VALUE_CHUNKS = 3
PAIR_ROWS = 2 * ROWS_DEV * G
NEG = -1e30
SHARD_AXES = ("ctx", "side")
SHARD_SIZES = (4, 2)
DP_AXES = ("z2", "z1", "z0", "y1", "y0")
NEAR_AXES = ("y1", "y0", "z0")
FAR_AXES = ("z2", "z1")
GATHER_AXES = ("z2", "z1", "z0", "y1", "y0")
UNIT_AXES = ("y1", "y0")
Z_AXES = ("z2", "z1", "z0")
HALF_AXES = ("z0",)
ATTEND_VMEM = 64 * 1024 * 1024

norm_eps = 1e-05
f32 = jnp.float32
bf16 = jnp.bfloat16


def bits_of(index, axes):
    return {a: index >> (len(axes) - 1 - i) & 1 for i, a in enumerate(axes)}


def gather_members():
    members = []
    for i in range(2 ** len(GATHER_AXES)):
        z, y = i % 8, (i + i // 8) % 4
        members.append({**bits_of(z, Z_AXES), **bits_of(y, UNIT_AXES)})
    return members


def near_members():
    members = []
    for i in range(2 ** len(NEAR_AXES)):
        members.append({**bits_of((i + i // 4) % 2, HALF_AXES), **bits_of(i % 4, UNIT_AXES)})
    return members


def index_of(bits, axes):
    index = 0
    for a in axes:
        index = index * 2 + bits[a]
    return index


def in_order(members, axes):
    names = DP_AXES + SHARD_AXES
    sizes = (2,) * len(DP_AXES) + SHARD_SIZES
    rest = [i for i, a in enumerate(names) if a not in axes]
    order = []
    for fixed in itertools.product(*(range(sizes[i]) for i in rest)):
        group = []
        for bits in members:
            device = 0
            for i, a in enumerate(names):
                device = device * sizes[i] + (bits[a] if a in bits else fixed[rest.index(i)])
            group.append(device)
        order.append(group)
    return order


def swap(x, members, axes):
    return lax.all_to_all(
        x, DP_AXES + SHARD_AXES, 0, 0, axis_index_groups=in_order(members, axes)
    )


def attend_kernel(
    table_hbm, lengths_hbm, q_hbm, nk_hbm, nv_hbm, key_hbm, value_hbm, out_ref,
    table, lengths, q_two, nk_ref, nv_ref, q_rows, keys, values, scores, weights, owner,
    small_sem, key_sem, value_sem,
):
    shard = lax.axis_index(SHARD_AXES)
    small = [
        pltpu.make_async_copy(src, dst, small_sem.at[i])
        for i, (src, dst) in enumerate(
            [(q_hbm, q_two), (nk_hbm, nk_ref), (nv_hbm, nv_ref), (table_hbm, table), (lengths_hbm, lengths)]
        )
    ]
    for one in small:
        one.start()
    key_step, value_step = TOKENS // KEY_CHUNKS, TOKENS // VALUE_CHUNKS
    key_copies = [
        pltpu.make_async_copy(
            key_hbm.at[pl.ds(c * key_step, key_step)],
            keys.at[pl.ds(c * key_step, key_step)],
            key_sem.at[c],
        )
        for c in range(KEY_CHUNKS)
    ]
    value_copies = [
        pltpu.make_async_copy(
            value_hbm.at[pl.ds(c * value_step, value_step)],
            values.at[pl.ds(c * value_step, value_step)],
            value_sem.at[c],
        )
        for c in range(VALUE_CHUNKS)
    ]
    for copy in key_copies:
        copy.start()
    for one in small:
        one.wait()
    for copy in value_copies:
        copy.start()

    for k in range(SLOTS):
        owner[table[0, 0, k]] = k

    def limits_of(slot):
        k = owner[slot]
        own = lax.div(k, PMAX)
        start = (lax.rem(k, PMAX) * 8 + shard) * PAGE
        return [jnp.where(own == r, lengths[r] - start, 0) for r in range(ROWS_DEV)]

    q_all = q_two[...].astype(f32)
    for h in range(KVH):
        for r in range(ROWS_DEV):
            for g in range(G):
                at = (h // 2) * PAIR_ROWS + r * 2 * G + (h % 2) * G + g
                n = h * G + g
                q_rows[at : at + 1, :] = q_all[r : r + 1, n * HD : (n + 1) * HD]
    row = lax.broadcasted_iota(jnp.int32, (PAIR_ROWS, HD), 0)
    second = lax.rem(lax.div(row, G), 2) == 1

    lane = lax.broadcasted_iota(jnp.int32, (2 * G, HD), 1)
    within = lax.rem(lane, PAGE)
    first_half = lane < PAGE
    bias = []
    for t in range(TOKENS // HD):
        left, right = limits_of(2 * t), limits_of(2 * t + 1)
        halves = [
            jnp.where(within < jnp.where(first_half, left[r], right[r]), 0.0, NEG)
            for r in range(ROWS_DEV)
        ]
        bias.append(jnp.concatenate(halves, axis=0))
    bias = jnp.concatenate(bias, axis=1)

    def per_group(ref, j):
        parts = []
        for r in range(ROWS_DEV):
            for h in (2 * j, 2 * j + 1):
                one = ref[r : r + 1, h * HD : (h + 1) * HD].astype(f32)
                parts.append(jnp.broadcast_to(one, (G, HD)))
        return jnp.concatenate(parts, axis=0)

    scale = 1.0 / math.sqrt(HD)
    wides = []
    for j in range(PAIRS):
        q = q_rows[j * PAIR_ROWS : (j + 1) * PAIR_ROWS, :]
        wides.append(
            jnp.concatenate([jnp.where(second, 0.0, q), jnp.where(second, q, 0.0)], axis=1).astype(
                bf16
            )
        )
    for c in range(KEY_CHUNKS):
        key_copies[c].wait()
        tokens = slice(c * key_step, (c + 1) * key_step)
        for j in range(PAIRS):
            scores[j * PAIR_ROWS : (j + 1) * PAIR_ROWS, tokens] = bias[:, tokens] + lax.dot_general(
                wides[j],
                keys[tokens, j * 2 * HD : (j + 1) * 2 * HD],
                (((1,), (1,)), ((), ())),
                preferred_element_type=f32,
            )
    stat_lane = lax.broadcasted_iota(jnp.int32, (PAIR_ROWS, HD), 1)
    added, stats = [], []
    for j in range(PAIRS):
        rows = slice(j * PAIR_ROWS, (j + 1) * PAIR_ROWS)
        fresh = jnp.sum(q_rows[rows, :] * per_group(nk_ref, j), axis=1, keepdims=True)
        fresh = jnp.where(shard == 0, fresh, NEG)
        peak = jnp.maximum(jnp.max(scores[rows, :], axis=1, keepdims=True), fresh)
        peak = jnp.maximum(peak, 0.1 * NEG)
        weight = jnp.exp((scores[rows, :] - peak) * scale)
        fresh_weight = jnp.exp((fresh - peak) * scale)
        total = jnp.sum(weight, axis=1, keepdims=True) + fresh_weight
        weights[rows, :] = weight.astype(bf16)
        own_stats = jnp.zeros((PAIR_ROWS, HD), f32)
        for n, value in enumerate((peak * scale, total)):
            rest = value
            for i in range(3):
                part = rest.astype(bf16).astype(f32)
                own_stats = jnp.where(stat_lane == 3 * n + i, part, own_stats)
                rest = rest - part
        stats.append(own_stats)
        added.append(fresh_weight * per_group(nv_ref, j))
    mixed = [jnp.zeros((PAIR_ROWS, 2 * HD), f32) for _ in range(PAIRS)]
    for c in range(VALUE_CHUNKS):
        value_copies[c].wait()
        tokens = slice(c * value_step, (c + 1) * value_step)
        for j in range(PAIRS):
            mixed[j] = mixed[j] + jnp.dot(
                weights[j * PAIR_ROWS : (j + 1) * PAIR_ROWS, tokens],
                values[tokens, j * 2 * HD : (j + 1) * 2 * HD],
                preferred_element_type=f32,
            )
    for j in range(PAIRS):
        for n in range(2):
            own, own_stats = [], []
            for r in range(ROWS_DEV):
                at = (2 * r + n) * G
                own.append(mixed[j][at : at + G, n * HD : (n + 1) * HD] + added[j][at : at + G, :])
                own_stats.append(stats[j][at : at + G, :])
            out_ref[2 * j + n, :, 0:HD] = jnp.concatenate(own, axis=0).astype(bf16)
            out_ref[2 * j + n, :, HD : 2 * HD] = jnp.concatenate(own_stats, axis=0).astype(bf16)


def attend(table, lengths, q, new_key, new_value, keys, values):
    vmem = pl.BlockSpec(memory_space=pltpu.VMEM)
    hbm = pl.BlockSpec(memory_space=pltpu.HBM)
    return pl.pallas_call(
        attend_kernel,
        out_shape=jax.ShapeDtypeStruct((KVH, ROWS_DEV * G, 2 * HD), bf16),
        in_specs=[hbm] * 7,
        out_specs=vmem,
        scratch_shapes=[
            pltpu.SMEM((1, 1, SLOTS), jnp.int32),
            pltpu.SMEM((ROWS_DEV,), jnp.int32),
            pltpu.VMEM((ROWS_DEV, KVH * G * HD), bf16),
            pltpu.VMEM((ROWS_DEV, KVH * HD), bf16),
            pltpu.VMEM((ROWS_DEV, KVH * HD), bf16),
            pltpu.VMEM((PAIRS * PAIR_ROWS, HD), f32),
            pltpu.VMEM((TOKENS, KVH * HD), bf16),
            pltpu.VMEM((TOKENS, KVH * HD), bf16),
            pltpu.VMEM((PAIRS * PAIR_ROWS, TOKENS), f32),
            pltpu.VMEM((PAIRS * PAIR_ROWS, TOKENS), bf16),
            pltpu.SMEM((SLOTS,), jnp.int32),
            pltpu.SemaphoreType.DMA((5,)),
            pltpu.SemaphoreType.DMA((KEY_CHUNKS,)),
            pltpu.SemaphoreType.DMA((VALUE_CHUNKS,)),
        ],
        compiler_params=pltpu.CompilerParams(vmem_limit_bytes=ATTEND_VMEM),
        name="attend",
    )(table, lengths, q, new_key, new_value, keys, values)


def merge_kernel(parts_ref, out_ref):
    shards = parts_ref.shape[0]
    peaks, totals = [], []
    for s in range(shards):
        stats = parts_ref[s, :, HD : 2 * HD].astype(f32)
        peaks.append(stats[:, 0:1] + stats[:, 1:2] + stats[:, 2:3])
        totals.append(stats[:, 3:4] + stats[:, 4:5] + stats[:, 5:6])
    peak = peaks[0]
    for s in range(1, shards):
        peak = jnp.maximum(peak, peaks[s])
    total = jnp.zeros_like(peak)
    mixed = jnp.zeros((ROWS_DEV * G, HD), f32)
    for s in range(shards):
        factor = jnp.exp(peaks[s] - peak)
        total = total + factor * totals[s]
        mixed = mixed + factor * parts_ref[s, :, 0:HD].astype(f32)
    attended = (mixed / total).astype(bf16)
    for i in range(out_ref.shape[0]):
        out_ref[i] = attended


def merge(parts, copies):
    vmem = pl.BlockSpec(memory_space=pltpu.VMEM)
    return pl.pallas_call(
        merge_kernel,
        out_shape=jax.ShapeDtypeStruct((copies, ROWS_DEV * G, HD), bf16),
        in_specs=[vmem],
        out_specs=vmem,
        compiler_params=pltpu.CompilerParams(vmem_limit_bytes=4 * 1024 * 1024),
        cost_estimate=pl.CostEstimate(flops=20_000_000_000, bytes_accessed=0, transcendentals=0),
        name="merge",
    )(parts)


def project_kernel(attended_ref, weight_ref, out_ref, rows_ref):
    groups = attended_ref.shape[0]
    for n in range(groups):
        at = index_of(gather_members()[n], DP_AXES) * ROWS_DEV * G
        rows_ref[at : at + ROWS_DEV * G, :] = attended_ref[n].astype(f32)
    heads = [rows_ref[pl.ds(g, groups * ROWS_DEV, stride=G), :] for g in range(G)]
    wide = jnp.concatenate(heads, axis=1).astype(bf16)
    result = jnp.dot(wide, weight_ref[...], preferred_element_type=f32).astype(bf16)
    for i in range(out_ref.shape[0]):
        out_ref[i] = result


def project(attended, weight, copies):
    groups = attended.shape[0]
    vmem = pl.BlockSpec(memory_space=pltpu.VMEM)
    return pl.pallas_call(
        project_kernel,
        out_shape=jax.ShapeDtypeStruct((copies, groups * ROWS_DEV, weight.shape[1]), bf16),
        in_specs=[vmem, vmem],
        out_specs=vmem,
        scratch_shapes=[pltpu.VMEM((groups * ROWS_DEV * G, HD), f32)],
        compiler_params=pltpu.CompilerParams(vmem_limit_bytes=8 * 1024 * 1024),
        cost_estimate=pl.CostEstimate(flops=20_000_000_000, bytes_accessed=0, transcendentals=0),
        name="project",
    )(attended, weight)


def widen_kernel(
    came_ref, residual_ref, gain_ref, gate_ref, up_ref, sent_ref, own_ref, middle_ref
):
    projected = came_ref[0].astype(f32)
    for s in range(1, came_ref.shape[0]):
        projected = projected + came_ref[s].astype(f32)
    middle = (residual_ref[...].astype(f32) + projected).astype(bf16).astype(f32)
    middle_ref[...] = middle
    share = own_ref.shape[0]
    at = pl.multiple_of(lax.axis_index(SHARD_AXES) * share, share)
    own_ref[...] = middle_ref[pl.ds(at, share), :]
    scaled = (middle * gain_ref[...]).astype(bf16)
    squares = jnp.sum(middle * middle, axis=1, keepdims=True)
    high = squares.astype(bf16).astype(f32)
    lane = lax.broadcasted_iota(jnp.int32, (middle.shape[0], HD), 1)
    tail = jnp.where(lane == 0, high, jnp.where(lane == 1, squares - high, 0.0)).astype(bf16)
    blocks = 2 ** len(UNIT_AXES)
    half = sent_ref.shape[1]
    units = gate_ref.shape[1] // blocks
    targets = near_members()
    for b in range(blocks):
        parts = [
            jnp.dot(
                scaled, weight_ref[:, b * units : (b + 1) * units], preferred_element_type=f32
            ).astype(bf16)
            for weight_ref in (gate_ref, up_ref)
        ]
        for i, bits in enumerate(targets):
            if index_of(bits, UNIT_AXES) != b:
                continue
            at = index_of(bits, HALF_AXES) * half
            for n in range(2):
                sent_ref[i, :, n * units : (n + 1) * units] = parts[n][at : at + half, :]
            sent_ref[i, :, 2 * units :] = tail[at : at + half, :]


def widen(came, residual, gain, gate_weight, up_weight, share):
    rows, width = residual.shape
    members, halves = 2 ** len(NEAR_AXES), 2 ** len(HALF_AXES)
    units = gate_weight.shape[1] * halves // members
    vmem = pl.BlockSpec(memory_space=pltpu.VMEM)
    return pl.pallas_call(
        widen_kernel,
        out_shape=(
            jax.ShapeDtypeStruct((members, rows // halves, 2 * units + HD), bf16),
            jax.ShapeDtypeStruct((share, width), f32),
        ),
        in_specs=[vmem] * 5,
        out_specs=(vmem, vmem),
        scratch_shapes=[pltpu.VMEM((rows, width), f32)],
        compiler_params=pltpu.CompilerParams(vmem_limit_bytes=8 * 1024 * 1024),
        name="widen",
    )(came, residual, gain, gate_weight, up_weight)


def finish_kernel(came_ref, out_ref):
    units = out_ref.shape[2]
    sums = came_ref[0].astype(f32)
    for n in range(1, came_ref.shape[0]):
        sums = sums + came_ref[n].astype(f32)
    squares = sums[:, 2 * units : 2 * units + 1] + sums[:, 2 * units + 1 : 2 * units + 2]
    inverse = 1.0 / jnp.sqrt(squares / D + norm_eps)
    gate = sums[:, :units] * inverse
    up = sums[:, units : 2 * units] * inverse
    hidden = (gate / (1.0 + jnp.exp(-gate)) * up).astype(bf16)
    for n in range(out_ref.shape[0]):
        out_ref[n] = hidden


def finish(came, copies):
    _, rows, wide = came.shape
    vmem = pl.BlockSpec(memory_space=pltpu.VMEM)
    return pl.pallas_call(
        finish_kernel,
        out_shape=jax.ShapeDtypeStruct((copies, rows, (wide - HD) // 2), bf16),
        in_specs=[vmem],
        out_specs=vmem,
        compiler_params=pltpu.CompilerParams(vmem_limit_bytes=4 * 1024 * 1024),
        name="finish",
    )(came)


def narrow_kernel(hidden_ref, down_ref, out_ref, rows_ref):
    groups, rows, units = hidden_ref.shape
    blocks = down_ref.shape[0] // units
    total = jnp.zeros(out_ref.shape, f32)
    for b in range(blocks):
        for i in range(groups):
            bits = gather_members()[i]
            if index_of(bits, UNIT_AXES) == b:
                at = index_of(bits, HALF_AXES + FAR_AXES) * rows
                rows_ref[b, at : at + rows, :] = hidden_ref[i].astype(f32)
        total = total + jnp.dot(
            rows_ref[b].astype(bf16),
            down_ref[b * units : (b + 1) * units, :],
            preferred_element_type=f32,
        )
    out_ref[...] = total.astype(bf16)


def narrow(hidden, down_weight):
    groups, rows, units = hidden.shape
    blocks = down_weight.shape[0] // units
    all_rows = rows * groups // blocks
    vmem = pl.BlockSpec(memory_space=pltpu.VMEM)
    return pl.pallas_call(
        narrow_kernel,
        out_shape=jax.ShapeDtypeStruct((all_rows, down_weight.shape[1]), bf16),
        in_specs=[vmem, vmem],
        out_specs=vmem,
        scratch_shapes=[pltpu.VMEM((blocks, all_rows, units), f32)],
        compiler_params=pltpu.CompilerParams(vmem_limit_bytes=8 * 1024 * 1024),
        name="narrow",
    )(hidden, down_weight)


def body(
    queries,
    new_key,
    new_value,
    key_pool,
    value_pool,
    page_table,
    lengths,
    residual,
    out_weight,
    norm_gain,
    gate_weight,
    up_weight,
    down_weight,
):
    shards = lax.axis_size(SHARD_AXES)
    groups = lax.axis_size(DP_AXES)
    far = lax.axis_size(FAR_AXES)
    rows, width = residual.shape
    share_rows = rows // shards

    parts = attend(
        page_table,
        lengths,
        queries,
        new_key,
        new_value,
        key_pool.reshape(TOKENS, KVH * HD),
        value_pool.reshape(TOKENS, KVH * HD),
    )
    attended = merge(lax.all_to_all(parts, SHARD_AXES, 0, 0), groups)
    attended = swap(attended, gather_members(), DP_AXES)
    came = lax.all_to_all(project(attended, out_weight, shards), SHARD_AXES, 0, 0)
    sent, middle_own = widen(
        came, residual, norm_gain.reshape(1, width), gate_weight, up_weight, share_rows
    )
    came = swap(sent, near_members(), NEAR_AXES)
    sent = jnp.sum(came.astype(f32), axis=0).astype(bf16)
    came = lax.all_to_all(sent.reshape(far, sent.shape[0] // far, sent.shape[1]), FAR_AXES, 0, 0)
    hidden = swap(finish(came, groups), gather_members(), GATHER_AXES)
    down = narrow(hidden, down_weight)
    down = lax.all_to_all(down.reshape(shards, share_rows, width), SHARD_AXES, 0, 0)
    return (middle_own + jnp.sum(down.astype(f32), axis=0)).astype(bf16)


def solution(mesh):
    lines, cores = mesh.shape["ctx"], mesh.shape["side"]
    split = Mesh(
        mesh.devices.reshape((2,) * len(DP_AXES) + (lines, cores)), DP_AXES + SHARD_AXES
    )
    dp, block = DP_AXES, SHARD_AXES
    placed = (
        P(dp, None),
        P(dp, None),
        P(dp, None),
        P(dp + block, None, None),
        P(dp + block, None, None),
        P(dp, block, None),
        P(dp),
        P(None, dp),
        P(block, dp),
        P(dp),
        P(dp, block),
        P(dp, block),
        P(block, dp),
    )
    return jax.shard_map(
        body, mesh=split, in_specs=placed, out_specs=P(block, dp), check_vma=False
    )
```

```python
import itertools
import math

import jax
import jax.numpy as jnp
from jax import lax
from jax.experimental import pallas as pl
from jax.experimental.pallas import tpu as pltpu
from jax.sharding import Mesh
from jax.sharding import PartitionSpec as P

D = 8192
KVH = 8
HD = 128
PAGE = 64
PMAX = 12
G = 8
ROWS_DEV = 2
SLOTS = ROWS_DEV * PMAX
TOKENS = SLOTS * PAGE
PAIRS = KVH // 2
KEY_CHUNKS = 3
VALUE_CHUNKS = 3
PAIR_ROWS = 2 * ROWS_DEV * G
NEG = -1e30
SHARD_AXES = ("ctx", "side")
SHARD_SIZES = (4, 2)
DP_AXES = ("z2", "z1", "z0", "y1", "y0")
NEAR_AXES = ("y1", "y0", "z0")
FAR_AXES = ("z2", "z1")
GATHER_AXES = ("z2", "z1", "z0", "y1", "y0")
UNIT_AXES = ("y1", "y0")
Z_AXES = ("z2", "z1", "z0")
HALF_AXES = ("z0",)
ATTEND_VMEM = 64 * 1024 * 1024

norm_eps = 1e-05
f32 = jnp.float32
bf16 = jnp.bfloat16


def bits_of(index, axes):
    return {a: index >> (len(axes) - 1 - i) & 1 for i, a in enumerate(axes)}


def gather_members():
    members = []
    for i in range(2 ** len(GATHER_AXES)):
        z, y = -i % 8, -(i + i // 8) % 4
        members.append({**bits_of(z, Z_AXES), **bits_of(y, UNIT_AXES)})
    return members


def index_of(bits, axes):
    index = 0
    for a in axes:
        index = index * 2 + bits[a]
    return index


def in_order(members, axes):
    names = DP_AXES + SHARD_AXES
    sizes = (2,) * len(DP_AXES) + SHARD_SIZES
    rest = [i for i, a in enumerate(names) if a not in axes]
    order = []
    for fixed in itertools.product(*(range(sizes[i]) for i in rest)):
        group = []
        for bits in members:
            device = 0
            for i, a in enumerate(names):
                device = device * sizes[i] + (bits[a] if a in bits else fixed[rest.index(i)])
            group.append(device)
        order.append(group)
    return order


def swap(x, members, axes):
    return lax.all_to_all(
        x, DP_AXES + SHARD_AXES, 0, 0, axis_index_groups=in_order(members, axes)
    )


def attend_kernel(
    table_hbm, lengths_hbm, q_hbm, nk_hbm, nv_hbm, key_hbm, value_hbm, out_ref,
    table, lengths, q_two, nk_ref, nv_ref, q_rows, keys, values, scores, weights, owner,
    small_sem, key_sem, value_sem,
):
    shard = lax.axis_index(SHARD_AXES)
    small = [
        pltpu.make_async_copy(src, dst, small_sem.at[i])
        for i, (src, dst) in enumerate(
            [(q_hbm, q_two), (nk_hbm, nk_ref), (nv_hbm, nv_ref), (table_hbm, table), (lengths_hbm, lengths)]
        )
    ]
    for one in small:
        one.start()
    key_step, value_step = TOKENS // KEY_CHUNKS, TOKENS // VALUE_CHUNKS
    key_copies = [
        pltpu.make_async_copy(
            key_hbm.at[pl.ds(c * key_step, key_step)],
            keys.at[pl.ds(c * key_step, key_step)],
            key_sem.at[c],
        )
        for c in range(KEY_CHUNKS)
    ]
    value_copies = [
        pltpu.make_async_copy(
            value_hbm.at[pl.ds(c * value_step, value_step)],
            values.at[pl.ds(c * value_step, value_step)],
            value_sem.at[c],
        )
        for c in range(VALUE_CHUNKS)
    ]
    for copy in key_copies:
        copy.start()
    for one in small:
        one.wait()
    for copy in value_copies:
        copy.start()

    for k in range(SLOTS):
        owner[table[0, 0, k]] = k

    def limits_of(slot):
        k = owner[slot]
        own = lax.div(k, PMAX)
        start = (lax.rem(k, PMAX) * 8 + shard) * PAGE
        return [jnp.where(own == r, lengths[r] - start, 0) for r in range(ROWS_DEV)]

    q_all = q_two[...].astype(f32)
    for h in range(KVH):
        for r in range(ROWS_DEV):
            for g in range(G):
                at = (h // 2) * PAIR_ROWS + r * 2 * G + (h % 2) * G + g
                n = h * G + g
                q_rows[at : at + 1, :] = q_all[r : r + 1, n * HD : (n + 1) * HD]
    row = lax.broadcasted_iota(jnp.int32, (PAIR_ROWS, HD), 0)
    second = lax.rem(lax.div(row, G), 2) == 1

    lane = lax.broadcasted_iota(jnp.int32, (2 * G, HD), 1)
    within = lax.rem(lane, PAGE)
    first_half = lane < PAGE
    bias = []
    for t in range(TOKENS // HD):
        left, right = limits_of(2 * t), limits_of(2 * t + 1)
        halves = [
            jnp.where(within < jnp.where(first_half, left[r], right[r]), 0.0, NEG)
            for r in range(ROWS_DEV)
        ]
        bias.append(jnp.concatenate(halves, axis=0))
    bias = jnp.concatenate(bias, axis=1)

    def per_group(ref, j):
        parts = []
        for r in range(ROWS_DEV):
            for h in (2 * j, 2 * j + 1):
                one = ref[r : r + 1, h * HD : (h + 1) * HD].astype(f32)
                parts.append(jnp.broadcast_to(one, (G, HD)))
        return jnp.concatenate(parts, axis=0)

    scale = 1.0 / math.sqrt(HD)
    wides = []
    for j in range(PAIRS):
        q = q_rows[j * PAIR_ROWS : (j + 1) * PAIR_ROWS, :]
        wides.append(
            jnp.concatenate([jnp.where(second, 0.0, q), jnp.where(second, q, 0.0)], axis=1).astype(
                bf16
            )
        )
    for c in range(KEY_CHUNKS):
        key_copies[c].wait()
        tokens = slice(c * key_step, (c + 1) * key_step)
        for j in range(PAIRS):
            scores[j * PAIR_ROWS : (j + 1) * PAIR_ROWS, tokens] = bias[:, tokens] + lax.dot_general(
                wides[j],
                keys[tokens, j * 2 * HD : (j + 1) * 2 * HD],
                (((1,), (1,)), ((), ())),
                preferred_element_type=f32,
            )
    stat_lane = lax.broadcasted_iota(jnp.int32, (PAIR_ROWS, HD), 1)
    added, stats = [], []
    for j in range(PAIRS):
        rows = slice(j * PAIR_ROWS, (j + 1) * PAIR_ROWS)
        fresh = jnp.sum(q_rows[rows, :] * per_group(nk_ref, j), axis=1, keepdims=True)
        fresh = jnp.where(shard == 0, fresh, NEG)
        peak = jnp.maximum(jnp.max(scores[rows, :], axis=1, keepdims=True), fresh)
        peak = jnp.maximum(peak, 0.1 * NEG)
        weight = jnp.exp((scores[rows, :] - peak) * scale)
        fresh_weight = jnp.exp((fresh - peak) * scale)
        total = jnp.sum(weight, axis=1, keepdims=True) + fresh_weight
        weights[rows, :] = weight.astype(bf16)
        own_stats = jnp.zeros((PAIR_ROWS, HD), f32)
        for n, value in enumerate((peak * scale, total)):
            rest = value
            for i in range(3):
                part = rest.astype(bf16).astype(f32)
                own_stats = jnp.where(stat_lane == 3 * n + i, part, own_stats)
                rest = rest - part
        stats.append(own_stats)
        added.append(fresh_weight * per_group(nv_ref, j))
    mixed = [jnp.zeros((PAIR_ROWS, 2 * HD), f32) for _ in range(PAIRS)]
    for c in range(VALUE_CHUNKS):
        value_copies[c].wait()
        tokens = slice(c * value_step, (c + 1) * value_step)
        for j in range(PAIRS):
            mixed[j] = mixed[j] + jnp.dot(
                weights[j * PAIR_ROWS : (j + 1) * PAIR_ROWS, tokens],
                values[tokens, j * 2 * HD : (j + 1) * 2 * HD],
                preferred_element_type=f32,
            )
    for j in range(PAIRS):
        for n in range(2):
            own, own_stats = [], []
            for r in range(ROWS_DEV):
                at = (2 * r + n) * G
                own.append(mixed[j][at : at + G, n * HD : (n + 1) * HD] + added[j][at : at + G, :])
                own_stats.append(stats[j][at : at + G, :])
            out_ref[2 * j + n, :, 0:HD] = jnp.concatenate(own, axis=0).astype(bf16)
            out_ref[2 * j + n, :, HD : 2 * HD] = jnp.concatenate(own_stats, axis=0).astype(bf16)


def attend(table, lengths, q, new_key, new_value, keys, values):
    vmem = pl.BlockSpec(memory_space=pltpu.VMEM)
    hbm = pl.BlockSpec(memory_space=pltpu.HBM)
    return pl.pallas_call(
        attend_kernel,
        out_shape=jax.ShapeDtypeStruct((KVH, ROWS_DEV * G, 2 * HD), bf16),
        in_specs=[hbm] * 7,
        out_specs=vmem,
        scratch_shapes=[
            pltpu.SMEM((1, 1, SLOTS), jnp.int32),
            pltpu.SMEM((ROWS_DEV,), jnp.int32),
            pltpu.VMEM((ROWS_DEV, KVH * G * HD), bf16),
            pltpu.VMEM((ROWS_DEV, KVH * HD), bf16),
            pltpu.VMEM((ROWS_DEV, KVH * HD), bf16),
            pltpu.VMEM((PAIRS * PAIR_ROWS, HD), f32),
            pltpu.VMEM((TOKENS, KVH * HD), bf16),
            pltpu.VMEM((TOKENS, KVH * HD), bf16),
            pltpu.VMEM((PAIRS * PAIR_ROWS, TOKENS), f32),
            pltpu.VMEM((PAIRS * PAIR_ROWS, TOKENS), bf16),
            pltpu.SMEM((SLOTS,), jnp.int32),
            pltpu.SemaphoreType.DMA((5,)),
            pltpu.SemaphoreType.DMA((KEY_CHUNKS,)),
            pltpu.SemaphoreType.DMA((VALUE_CHUNKS,)),
        ],
        compiler_params=pltpu.CompilerParams(vmem_limit_bytes=ATTEND_VMEM),
        name="attend",
    )(table, lengths, q, new_key, new_value, keys, values)


def merge_kernel(parts_ref, out_ref):
    shards = parts_ref.shape[0]
    peaks, totals = [], []
    for s in range(shards):
        stats = parts_ref[s, :, HD : 2 * HD].astype(f32)
        peaks.append(stats[:, 0:1] + stats[:, 1:2] + stats[:, 2:3])
        totals.append(stats[:, 3:4] + stats[:, 4:5] + stats[:, 5:6])
    peak = peaks[0]
    for s in range(1, shards):
        peak = jnp.maximum(peak, peaks[s])
    total = jnp.zeros_like(peak)
    mixed = jnp.zeros((ROWS_DEV * G, HD), f32)
    for s in range(shards):
        factor = jnp.exp(peaks[s] - peak)
        total = total + factor * totals[s]
        mixed = mixed + factor * parts_ref[s, :, 0:HD].astype(f32)
    attended = (mixed / total).astype(bf16)
    for i in range(out_ref.shape[0]):
        out_ref[i] = attended


def merge(parts, copies):
    vmem = pl.BlockSpec(memory_space=pltpu.VMEM)
    return pl.pallas_call(
        merge_kernel,
        out_shape=jax.ShapeDtypeStruct((copies, ROWS_DEV * G, HD), bf16),
        in_specs=[vmem],
        out_specs=vmem,
        compiler_params=pltpu.CompilerParams(vmem_limit_bytes=4 * 1024 * 1024),
        cost_estimate=pl.CostEstimate(flops=20_000_000_000, bytes_accessed=0, transcendentals=0),
        name="merge",
    )(parts)


def project_kernel(attended_ref, weight_ref, out_ref, rows_ref):
    groups = attended_ref.shape[0]
    for n in range(groups):
        rows_ref[n * ROWS_DEV * G : (n + 1) * ROWS_DEV * G, :] = attended_ref[n].astype(f32)
    heads = [rows_ref[pl.ds(g, groups * ROWS_DEV, stride=G), :] for g in range(G)]
    wide = jnp.concatenate(heads, axis=1).astype(bf16)
    result = jnp.dot(wide, weight_ref[...], preferred_element_type=f32).astype(bf16)
    for i in range(out_ref.shape[0]):
        out_ref[i] = result


def project(attended, weight, copies):
    groups = attended.shape[0]
    vmem = pl.BlockSpec(memory_space=pltpu.VMEM)
    return pl.pallas_call(
        project_kernel,
        out_shape=jax.ShapeDtypeStruct((copies, groups * ROWS_DEV, weight.shape[1]), bf16),
        in_specs=[vmem, vmem],
        out_specs=vmem,
        scratch_shapes=[pltpu.VMEM((groups * ROWS_DEV * G, HD), f32)],
        compiler_params=pltpu.CompilerParams(vmem_limit_bytes=8 * 1024 * 1024),
        cost_estimate=pl.CostEstimate(flops=20_000_000_000, bytes_accessed=0, transcendentals=0),
        name="project",
    )(attended, weight)


def widen_kernel(
    came_ref, residual_ref, gain_ref, gate_ref, up_ref, sent_ref, own_ref, middle_ref
):
    projected = came_ref[0].astype(f32)
    for s in range(1, came_ref.shape[0]):
        projected = projected + came_ref[s].astype(f32)
    middle = (residual_ref[...].astype(f32) + projected).astype(bf16).astype(f32)
    middle_ref[...] = middle
    share = own_ref.shape[0]
    at = pl.multiple_of(lax.axis_index(SHARD_AXES) * share, share)
    own_ref[...] = middle_ref[pl.ds(at, share), :]
    scaled = (middle * gain_ref[...]).astype(bf16)
    squares = jnp.sum(middle * middle, axis=1, keepdims=True)
    high = squares.astype(bf16).astype(f32)
    lane = lax.broadcasted_iota(jnp.int32, (middle.shape[0], HD), 1)
    tail = jnp.where(lane == 0, high, jnp.where(lane == 1, squares - high, 0.0)).astype(bf16)
    blocks = 2 ** len(UNIT_AXES)
    half = sent_ref.shape[1]
    units = gate_ref.shape[1] // blocks
    targets = [bits_of(i, NEAR_AXES) for i in range(sent_ref.shape[0])]
    for b in range(blocks):
        parts = [
            jnp.dot(
                scaled, weight_ref[:, b * units : (b + 1) * units], preferred_element_type=f32
            ).astype(bf16)
            for weight_ref in (gate_ref, up_ref)
        ]
        for i, bits in enumerate(targets):
            if index_of(bits, UNIT_AXES) != b:
                continue
            at = index_of(bits, HALF_AXES) * half
            for n in range(2):
                sent_ref[i, :, n * units : (n + 1) * units] = parts[n][at : at + half, :]
            sent_ref[i, :, 2 * units :] = tail[at : at + half, :]


def widen(came, residual, gain, gate_weight, up_weight, share):
    rows, width = residual.shape
    members, halves = 2 ** len(NEAR_AXES), 2 ** len(HALF_AXES)
    units = gate_weight.shape[1] * halves // members
    vmem = pl.BlockSpec(memory_space=pltpu.VMEM)
    return pl.pallas_call(
        widen_kernel,
        out_shape=(
            jax.ShapeDtypeStruct((members, rows // halves, 2 * units + HD), bf16),
            jax.ShapeDtypeStruct((share, width), f32),
        ),
        in_specs=[vmem] * 5,
        out_specs=(vmem, vmem),
        scratch_shapes=[pltpu.VMEM((rows, width), f32)],
        compiler_params=pltpu.CompilerParams(vmem_limit_bytes=8 * 1024 * 1024),
        name="widen",
    )(came, residual, gain, gate_weight, up_weight)


def finish_kernel(came_ref, out_ref):
    units = out_ref.shape[2]
    sums = came_ref[0].astype(f32)
    for n in range(1, came_ref.shape[0]):
        sums = sums + came_ref[n].astype(f32)
    squares = sums[:, 2 * units : 2 * units + 1] + sums[:, 2 * units + 1 : 2 * units + 2]
    inverse = 1.0 / jnp.sqrt(squares / D + norm_eps)
    gate = sums[:, :units] * inverse
    up = sums[:, units : 2 * units] * inverse
    hidden = (gate / (1.0 + jnp.exp(-gate)) * up).astype(bf16)
    for n in range(out_ref.shape[0]):
        out_ref[n] = hidden


def finish(came, copies):
    _, rows, wide = came.shape
    vmem = pl.BlockSpec(memory_space=pltpu.VMEM)
    return pl.pallas_call(
        finish_kernel,
        out_shape=jax.ShapeDtypeStruct((copies, rows, (wide - HD) // 2), bf16),
        in_specs=[vmem],
        out_specs=vmem,
        compiler_params=pltpu.CompilerParams(vmem_limit_bytes=4 * 1024 * 1024),
        name="finish",
    )(came)


def narrow_kernel(hidden_ref, down_ref, out_ref, rows_ref):
    groups, rows, units = hidden_ref.shape
    blocks = down_ref.shape[0] // units
    total = jnp.zeros(out_ref.shape, f32)
    for b in range(blocks):
        for i in range(groups):
            bits = gather_members()[i]
            if index_of(bits, UNIT_AXES) == b:
                at = index_of(bits, HALF_AXES + FAR_AXES) * rows
                rows_ref[b, at : at + rows, :] = hidden_ref[i].astype(f32)
        total = total + jnp.dot(
            rows_ref[b].astype(bf16),
            down_ref[b * units : (b + 1) * units, :],
            preferred_element_type=f32,
        )
    out_ref[...] = total.astype(bf16)


def narrow(hidden, down_weight):
    groups, rows, units = hidden.shape
    blocks = down_weight.shape[0] // units
    all_rows = rows * groups // blocks
    vmem = pl.BlockSpec(memory_space=pltpu.VMEM)
    return pl.pallas_call(
        narrow_kernel,
        out_shape=jax.ShapeDtypeStruct((all_rows, down_weight.shape[1]), bf16),
        in_specs=[vmem, vmem],
        out_specs=vmem,
        scratch_shapes=[pltpu.VMEM((blocks, all_rows, units), f32)],
        compiler_params=pltpu.CompilerParams(vmem_limit_bytes=8 * 1024 * 1024),
        name="narrow",
    )(hidden, down_weight)


def body(
    queries,
    new_key,
    new_value,
    key_pool,
    value_pool,
    page_table,
    lengths,
    residual,
    out_weight,
    norm_gain,
    gate_weight,
    up_weight,
    down_weight,
):
    shards = lax.axis_size(SHARD_AXES)
    groups = lax.axis_size(DP_AXES)
    far = lax.axis_size(FAR_AXES)
    rows, width = residual.shape
    share_rows = rows // shards

    parts = attend(
        page_table,
        lengths,
        queries,
        new_key,
        new_value,
        key_pool.reshape(TOKENS, KVH * HD),
        value_pool.reshape(TOKENS, KVH * HD),
    )
    attended = merge(lax.all_to_all(parts, SHARD_AXES, 0, 0), groups)
    attended = lax.all_to_all(attended, DP_AXES, 0, 0)
    came = lax.all_to_all(project(attended, out_weight, shards), SHARD_AXES, 0, 0)
    sent, middle_own = widen(
        came, residual, norm_gain.reshape(1, width), gate_weight, up_weight, share_rows
    )
    came = lax.all_to_all(sent, NEAR_AXES, 0, 0)
    sent = jnp.sum(came.astype(f32), axis=0).astype(bf16)
    came = lax.all_to_all(sent.reshape(far, sent.shape[0] // far, sent.shape[1]), FAR_AXES, 0, 0)
    hidden = swap(finish(came, groups), gather_members(), GATHER_AXES)
    down = narrow(hidden, down_weight)
    down = lax.all_to_all(down.reshape(shards, share_rows, width), SHARD_AXES, 0, 0)
    return (middle_own + jnp.sum(down.astype(f32), axis=0)).astype(bf16)


def solution(mesh):
    lines, cores = mesh.shape["ctx"], mesh.shape["side"]
    split = Mesh(
        mesh.devices.reshape((2,) * len(DP_AXES) + (lines, cores)), DP_AXES + SHARD_AXES
    )
    dp, block = DP_AXES, SHARD_AXES
    placed = (
        P(dp, None),
        P(dp, None),
        P(dp, None),
        P(dp + block, None, None),
        P(dp + block, None, None),
        P(dp, block, None),
        P(dp),
        P(None, dp),
        P(block, dp),
        P(dp),
        P(dp, block),
        P(dp, block),
        P(block, dp),
    )
    return jax.shard_map(
        body, mesh=split, in_specs=placed, out_specs=P(block, dp), check_vma=False
    )
```
